256 devices in a mesh: dp: 4 (over x), ep: 64 (over y, z, core).
Axes of the slice: x: 4, y: 4, z: 8, core: 2. Of those that a mesh axis runs over, the one named last changes fastest.
Arguments:
- tokens: bfloat16 [4, 2048, 2048], P('dp', 'ep'), may hold values from -12 to 12
- cotangent: bfloat16 [4, 2048, 2048], P('dp', 'ep'), may hold values from -6 to 6
- assign: int32 [4, 2048, 8], P('dp', 'ep'), may hold values from 0 to 63, as said below
- w_router: bfloat16 [2048, 64], replicated, may hold values from -0.125 to 0.125
- w_gate: bfloat16 [64, 2048, 768], P('ep'), may hold values from -0.125 to 0.125
- w_up: bfloat16 [64, 2048, 768], P('ep'), may hold values from -0.125 to 0.125
- w_down: bfloat16 [64, 2048, 768], P('ep'), may hold values from -0.21875 to 0.21875
Outputs:
- grad_tokens: bfloat16 [4, 2048, 2048], P('dp', 'ep')
- grad_router: float32 [2048, 64], replicated
- grad_gate: bfloat16 [64, 2048, 768], P('ep', 'dp')
- grad_up: bfloat16 [64, 2048, 768], P('ep', 'dp')
- grad_down: bfloat16 [64, 2048, 768], P('ep', 'dp')
The draws below stay inside these ranges and needn't reach their ends.
Inputs may be any that keep to these rules, and one draw needn't show every extreme that they name: `assign`: each token names 8 different experts; the routes of the 32 tokens of one device name one expert at most 8 times, and in every draw one expert is named exactly 8 times by the routes of every device.
All inputs are finite; a program needn't handle non-finite values.
Results may differ from the reference program's by a relative error of at most 0.015.
Values may be sent and summed in bfloat16 or wider, within the bound.
A program may use at most 128 MiB of HBM per device.

```python
import jax
import jax.numpy as jnp
from jax import lax

D = 2048
FF = 768
TOP = 8
ITERS = 3
TOK_DEV = 32
EXPERTS = 64
REP_TOK = 2048
SLOT = 8
N_DP = 4
N_EP = 64


def route_block(block_key, hot_expert):
    first_key, second_key, third_key, fourth_key = jax.random.split(block_key, 4)
    others_count = EXPERTS - 1
    other_order = jax.random.permutation(first_key, others_count).astype(jnp.int32)
    others = other_order + (other_order >= hot_expert).astype(jnp.int32)
    routes_total = TOK_DEV * TOP
    remaining = routes_total - SLOT
    base_count = remaining // others_count
    extra_count = remaining % others_count
    counts = base_count + (jnp.arange(others_count, dtype=jnp.int32) < extra_count).astype(jnp.int32)
    move_limit = max(0, min(base_count, SLOT - base_count - 1))
    pair_count = others_count // 2
    move_sizes = jax.random.randint(second_key, (pair_count,), 0, move_limit + 1).astype(jnp.int32)
    count_shift = jnp.zeros((others_count,), jnp.int32)
    count_shift = count_shift.at[0:2 * pair_count:2].add(-move_sizes).at[1:2 * pair_count:2].add(move_sizes)
    counts = counts + count_shift
    experts_all = jnp.concatenate([jnp.full((1,), hot_expert, jnp.int32), others])
    counts_all = jnp.concatenate([jnp.full((1,), SLOT, jnp.int32), counts])
    shuffle = jax.random.permutation(third_key, EXPERTS)
    experts_all = experts_all[shuffle]
    counts_all = counts_all[shuffle]
    run_bounds = jnp.cumsum(counts_all)
    position = jnp.arange(routes_total, dtype=jnp.int32)
    run_index = jnp.sum((run_bounds[None, :] <= position[:, None]).astype(jnp.int32), axis=1)
    sequence = experts_all[run_index]
    route_table = sequence.reshape(TOP, TOK_DEV).T
    return route_table[jax.random.permutation(fourth_key, TOK_DEV)]


def draw_assign(key, part):
    hot_expert = jax.random.randint(jax.random.fold_in(key, 11), (), 0, EXPERTS).astype(jnp.int32)
    block_keys = jax.random.split(jax.random.fold_in(key, 12), N_DP * (REP_TOK // TOK_DEV))
    blocks = jax.vmap(lambda block_key: route_block(block_key, hot_expert))(block_keys)
    return blocks.reshape(N_DP, REP_TOK, TOP).astype(jnp.int32)


def draw_tokens(key, part):
    noise_key = jax.random.fold_in(key, 21)
    drift_key = jax.random.fold_in(key, 22)
    noise_field = jax.random.normal(noise_key, (N_DP, REP_TOK, D), jnp.float32)
    drift_field = jax.random.normal(drift_key, (N_DP, 1, D), jnp.float32)
    ramp_profile = (jnp.arange(REP_TOK, dtype=jnp.float32) / REP_TOK)[None, :, None]
    return jnp.clip(noise_field + 1.5 * ramp_profile * drift_field, -12.0, 12.0).astype(jnp.bfloat16)


def level_of(stream_key, shape, cuts, least, largest):
    gain, own = 1.0, jax.random.fold_in(stream_key, 6)
    for dim, blocks in cuts:
        draws = jnp.exp(jax.random.uniform(jax.random.fold_in(own, dim), (blocks,), jnp.float32, least / len(cuts), largest / len(cuts)))
        gain = gain * jnp.repeat(draws, shape[dim] // blocks).reshape([-1 if axis == dim else 1 for axis in range(len(shape))])
    return gain


def gaussian(key, extent, deviation, bound, shards=(), held_as=jnp.bfloat16):
    factor_of = level_of(key, extent, shards, -0.22, 0.18) if shards else 1.0
    values = jax.random.normal(key, extent, jnp.float32) * deviation * factor_of
    return jnp.minimum(jnp.maximum(values, -bound), bound).astype(held_as)


def setup_inputs(seed: int = 0) -> dict:
    arg_keys = jax.random.split(jax.random.key(seed), 8)
    tokens = draw_tokens(jax.random.fold_in(arg_keys[7], 71), 0)
    cotangent = gaussian(arg_keys[1], (N_DP, REP_TOK, D), 1.0, 6.0, ((0, 4), (1, 64)))
    assign = draw_assign(jax.random.fold_in(arg_keys[7], 71), 0)
    w_router = gaussian(arg_keys[3], (D, EXPERTS), D ** -0.5, 0.125)
    w_gate = gaussian(arg_keys[4], (EXPERTS, D, FF), D ** -0.5, 0.125, ((0, 64),))
    w_up = gaussian(arg_keys[5], (EXPERTS, D, FF), D ** -0.5, 0.125, ((0, 64),))
    w_down = gaussian(arg_keys[6], (EXPERTS, D, FF), FF ** -0.5, 0.21875, ((0, 64),))
    return dict(tokens=tokens, cotangent=cotangent, assign=assign, w_router=w_router, w_gate=w_gate, w_up=w_up, w_down=w_down)


cos_scale = 48.0
eps_norm = 1e-06
contract_first = (((0,), (0,)), ((), ()))
contract_last = (((1,), (1,)), ((), ()))

def logit_map(flat_tokens, router):
    inner_products = jnp.dot(flat_tokens, router, precision=lax.Precision.HIGHEST)
    token_norm = jnp.sqrt(lax.optimization_barrier(jnp.sum(flat_tokens * flat_tokens, axis=1)) + eps_norm)
    column_norm = jnp.sqrt(lax.optimization_barrier(jnp.sum(router * router, axis=0)) + eps_norm)
    return cos_scale * inner_products / (token_norm[:, None] * column_norm[None, :])

def expert_backward(expert_rows, expert_cotangent, rows_gate, gate_matrix, up_matrix, down_matrix):
    gate_linear = jnp.dot(expert_rows, gate_matrix, preferred_element_type=jnp.float32)
    up_linear = jnp.dot(expert_rows, up_matrix, preferred_element_type=jnp.float32)
    sigmoid_gate = jax.nn.sigmoid(gate_linear)
    activation = gate_linear * sigmoid_gate
    product = activation * up_linear
    hidden = product.astype(jnp.bfloat16)
    weighted = (rows_gate[:, None] * product).astype(jnp.bfloat16)
    raw_back = jnp.dot(expert_cotangent, down_matrix, preferred_element_type=jnp.float32)
    gate_grad = lax.optimization_barrier(jnp.sum(raw_back * hidden.astype(jnp.float32), axis=1)).astype(jnp.bfloat16)
    scaled_back = rows_gate[:, None] * raw_back
    up_delta = (scaled_back * activation).astype(jnp.bfloat16)
    gate_delta = (scaled_back * up_linear * sigmoid_gate * (1.0 + gate_linear * (1.0 - sigmoid_gate))).astype(jnp.bfloat16)
    route_back = (lax.dot_general(gate_delta, gate_matrix, contract_last, preferred_element_type=jnp.float32) + lax.dot_general(up_delta, up_matrix, contract_last, preferred_element_type=jnp.float32)).astype(jnp.bfloat16)
    return (gate_grad, route_back, gate_delta, up_delta, weighted)

def reference(tokens, cotangent, assign, w_router, w_gate, w_up, w_down):
    replica_count, token_count, model_width = tokens.shape
    experts = w_router.shape[1]
    per_token = assign.shape[2]
    flat_tokens = tokens.reshape(-1, model_width).astype(jnp.float32)
    logits_flat, logit_vjp = jax.vjp(logit_map, flat_tokens, w_router.astype(jnp.float32))
    logits = logits_flat.reshape(replica_count, token_count, experts)
    kernel_start = jnp.exp(logits)
    kernel = kernel_start
    saved_steps = []
    for sweep_index in range(ITERS):
        column = lax.optimization_barrier(jnp.sum(kernel, axis=1, keepdims=True))
        scaled = kernel / column
        row_total = lax.optimization_barrier(jnp.sum(scaled, axis=2, keepdims=True))
        kernel = scaled / row_total
        saved_steps.append((column, scaled, row_total, kernel))
    expert_ids = jnp.arange(experts, dtype=jnp.int32)
    onehot = (assign[..., None] == expert_ids).astype(jnp.float32)
    picked = lax.optimization_barrier(jnp.sum(onehot * kernel[:, :, None, :], axis=3))
    picked_sum = lax.optimization_barrier(jnp.sum(picked, axis=2, keepdims=True))
    gates = picked / picked_sum
    gate_half = gates.astype(jnp.bfloat16)
    routes_total = replica_count * token_count * per_token
    flat_assign = assign.reshape(-1).astype(jnp.int32)
    route_order = jnp.argsort(flat_assign, stable=True).astype(jnp.int32)
    counts = lax.optimization_barrier(jnp.sum((flat_assign[:, None] == expert_ids).astype(jnp.int32), axis=0))
    starts = (jnp.cumsum(counts) - counts).astype(jnp.int32)
    capacity = N_DP * N_EP * SLOT
    padded_order = jnp.concatenate([route_order, jnp.zeros((capacity,), jnp.int32)])
    token_rows = tokens.reshape(-1, model_width)
    cotangent_rows = cotangent.reshape(-1, model_width)
    gate_flat = gate_half.reshape(-1).astype(jnp.float32)

    def per_expert(totals, expert):
        back_total, gate_total = totals
        route_index = lax.dynamic_slice(padded_order, (starts[expert],), (capacity,)).astype(jnp.int32)
        valid_rows = jnp.arange(capacity, dtype=jnp.int32) < counts[expert]
        token_index = (route_index // per_token).astype(jnp.int32)
        zero_half = jnp.zeros((), jnp.bfloat16)
        expert_rows = jnp.where(valid_rows[:, None], token_rows[token_index], zero_half)
        expert_cotangent = jnp.where(valid_rows[:, None], cotangent_rows[token_index], zero_half)
        rows_gate = jnp.where(valid_rows, gate_flat[route_index], 0.0)
        gate_grad, route_back, gate_delta, up_delta, weighted = expert_backward(expert_rows, expert_cotangent, rows_gate, w_gate[expert], w_up[expert], w_down[expert])
        grad_g = lax.dot_general(expert_rows, gate_delta, contract_first, preferred_element_type=jnp.float32).astype(jnp.bfloat16)
        grad_u = lax.dot_general(expert_rows, up_delta, contract_first, preferred_element_type=jnp.float32).astype(jnp.bfloat16)
        grad_d = lax.dot_general(expert_cotangent, weighted, contract_first, preferred_element_type=jnp.float32).astype(jnp.bfloat16)
        back_total = back_total.at[token_index].add(jnp.where(valid_rows[:, None], route_back.astype(jnp.float32), 0.0))
        gate_total = gate_total.at[route_index].add(jnp.where(valid_rows, gate_grad.astype(jnp.float32), 0.0))
        return ((back_total, gate_total), (grad_g, grad_u, grad_d))
    initial = (jnp.zeros((replica_count * token_count, model_width), jnp.float32), jnp.zeros((routes_total,), jnp.float32))
    (expert_back, gate_total), (grad_gate, grad_up, grad_down) = lax.scan(per_expert, initial, expert_ids)
    route_grad = gate_total.reshape(replica_count, token_count, per_token)
    picked_grad = (route_grad - lax.optimization_barrier(jnp.sum(route_grad * gates, axis=2, keepdims=True))) / picked_sum
    kernel_grad = lax.optimization_barrier(jnp.sum(onehot * picked_grad[..., None], axis=2))
    for sweep_index in reversed(range(ITERS)):
        column, scaled, row_total, kernel_step = saved_steps[sweep_index]
        scaled_grad = (kernel_grad - lax.optimization_barrier(jnp.sum(kernel_grad * kernel_step, axis=2, keepdims=True))) / row_total
        kernel_grad = (scaled_grad - lax.optimization_barrier(jnp.sum(scaled_grad * scaled, axis=1, keepdims=True))) / column
    logit_grad = kernel_grad * kernel_start
    router_back, grad_router = logit_vjp(logit_grad.reshape(-1, experts))
    grad_tokens = (expert_back + router_back).astype(jnp.bfloat16).reshape(tokens.shape)
    return (grad_tokens, grad_router, grad_gate, grad_up, grad_down)
```

```python
import functools
import heapq

import jax
import jax.numpy as jnp
from jax import lax
from jax.experimental import pallas as pl
from jax.experimental.pallas import tpu as pltpu
from jax.sharding import PartitionSpec as P

ITERS = 3
SLOTS = 8
LANES = 128
GROUP = 256
MESH = pl.DeviceIdType.MESH
f32 = jnp.float32
bf16 = jnp.bfloat16

cos_scale = 48.0
eps_norm = 1e-06
contract_first = (((0,), (0,)), ((), ()))
contract_last = (((1,), (1,)), ((), ()))


def torus_of(ep):
    ny = 4
    return ny, ep // (2 * ny)


def gather_plan(ny, nz, unit_us=2.7, mate_us=0.5, hop_us=1.0):
    def half(part, side):
        return side if part is None else (part if part == side else -1)

    def spread(which, a, b, part):
        na, nb = (nz, ny) if which == 0 else (ny, nz)
        out = []

        def along(axis, n, at, signs):
            for sign in signs:
                last = abs(at) + 1 == n // 2
                piece = half(part, 0 if sign > 0 else 1) if last else part
                if piece != -1:
                    out.append((axis, sign, piece))

        def onward(at, n):
            if at == 0:
                return (1, -1)
            return ((1,) if at > 0 else (-1,)) if abs(at) < n // 2 else ()

        if b == 0:
            along(0, na, a, onward(a, na))
        along(1, nb, b, onward(b, nb))
        return out

    heap, order, free, steps, ids = [], 0, {}, [], 0
    for which in (0, 1):
        heapq.heappush(heap, (0.0, order, None, which, 0, 0, None))
        order += 1
    while heap:
        now, _, arrival, which, a, b, part = heapq.heappop(heap)
        dy, dz = (b, a) if which == 0 else (a, b)
        sends = []
        for axis, sign, piece in spread(which, a, b, part):
            link = "zy"[axis] if which == 0 else "yz"[axis]
            share = 1.0 if piece is None else 0.5
            end = max(now, free.get((link, sign), 0.0)) + unit_us * share
            free[(link, sign)] = end
            na, nb = (a + sign, b) if axis == 0 else (a, b + sign)
            heapq.heappush(heap, (end + hop_us, order, ids, which, na, nb, piece))
            sends.append((ids, which, dy, dz, part if piece is None else piece, link, sign))
            order += 1
            ids += 1
        sends.append((ids, which, dy, dz, part, "mate", 0))
        ids += 1
        steps.append((None if arrival is None else (arrival, which, dy, dz, part), sends))
    return steps, ids


def place(ep, ny, nz):
    me = lax.axis_index("ep")
    core = lax.rem(me, 2)
    chip = me // 2
    return me, core, chip // nz, lax.rem(chip, nz)


def at_ep(nz, y, z, core):
    return (y * nz + z) * 2 + core


def enter(peers):
    barrier = pltpu.get_barrier_semaphore()
    for peer in peers:
        pl.semaphore_signal(barrier, inc=1, device_id=peer, device_id_type=MESH)
    pl.semaphore_wait(barrier, len(peers))


def dispatch_kernel(
    ep,
    tok_ref,
    cot_ref,
    assign_ref,
    router_ref,
    rows_tok,
    rows_cot,
    rows_gate,
    pick_out,
    kernels_out,
    columns_out,
    totals_out,
    logits_out,
    marks_out,
    slice_out,
    tok_all,
    cot_all,
    meta,
    row_mask,
    row_gate,
    meta_send,
    meta_recv,
    send_sem,
    recv_sem,
):
    ny, nz = torus_of(ep)
    count, width = tok_ref.shape
    experts = router_ref.shape[1]
    groups = ep * count // GROUP
    per_group = GROUP // count
    dp = lax.axis_index("dp")
    me, core, y, z = place(ep, ny, nz)
    mate = (dp, at_ep(nz, y, z, 1 - core))
    z_peers = [(dp, at_ep(nz, y, lax.rem(z + k, nz), core)) for k in range(1, nz)]
    y_peers = [(dp, at_ep(nz, lax.rem(y + k, ny), z, core)) for k in range(1, ny)]
    enter([mate, *z_peers, *y_peers])

    local = tok_ref[...]
    router = router_ref[...]
    wide = local.astype(f32)
    inverse_token = 1.0 / jnp.sqrt(jnp.sum(wide * wide, axis=1, keepdims=True) + eps_norm)
    router_wide = router.astype(f32)
    column_norm = jnp.sqrt(jnp.sum(router_wide * router_wide, axis=0, keepdims=True) + eps_norm)
    inner = jnp.dot(local, router, preferred_element_type=f32)
    logits = cos_scale * inner * inverse_token / column_norm
    ids = lax.broadcasted_iota(jnp.int32, (count, experts), 1)
    routes = assign_ref[...]
    hit = jnp.zeros((count, experts), f32)
    for k in range(routes.shape[1]):
        hit = jnp.where(routes[:, k : k + 1] == ids, inverse_token, hit)
    mine = y * nz + z
    meta[core, mine] = jnp.concatenate([logits, hit], axis=1)
    tok_all[me] = local
    cot_all[me] = cot_ref[...]

    def meta_copy(n, part, peer):
        return pltpu.make_async_remote_copy(
            src_ref=part, dst_ref=part, send_sem=meta_send.at[n], recv_sem=meta_recv.at[n],
            device_id=peer, device_id_type=MESH,
        )

    def meta_part(c, block, blocks):
        return meta.at[c, pl.ds(block, blocks)]

    z_copies = [meta_copy(k, meta_part(core, mine, 1), p) for k, p in enumerate(z_peers)]
    for copy in z_copies:
        copy.start()

    steps, total = gather_plan(ny, nz)
    ends = {
        ("z", 1): (dp, at_ep(nz, y, lax.rem(z + 1, nz), core)),
        ("z", -1): (dp, at_ep(nz, y, lax.rem(z + nz - 1, nz), core)),
        ("y", 1): (dp, at_ep(nz, lax.rem(y + 1, ny), z, core)),
        ("y", -1): (dp, at_ep(nz, lax.rem(y + ny - 1, ny), z, core)),
        ("mate", 0): mate,
    }
    tables = (tok_all, cot_all)

    def view(which, dy, dz, part, c):
        block = at_ep(nz, lax.rem(y - dy + 2 * ny, ny), lax.rem(z - dz + 2 * nz, nz), c)
        first, rows = (0, count) if part is None else (part * (count // 2), count // 2)
        return tables[which].at[block, pl.ds(first, rows)]

    def block_copy(n, ref, end):
        return pltpu.make_async_remote_copy(
            src_ref=ref, dst_ref=ref, send_sem=send_sem.at[n], recv_sem=recv_sem.at[n],
            device_id=ends[end], device_id_type=MESH,
        )

    started, mate_arrivals = [], []

    def run(step):
        arrival, sends = step
        if arrival is not None:
            n, which, dy, dz, part = arrival
            block_copy(n, view(which, dy, dz, part, core), ("z", 1)).wait_recv()
        for n, which, dy, dz, part, link, sign in sends:
            copy = block_copy(n, view(which, dy, dz, part, core), (link, sign))
            copy.start()
            started.append(copy)
            if link == "mate":
                mate_arrivals.append((n, which, dy, dz, part))

    def balance():
        for g in range(groups):
            blocks = []
            for b in range(g * per_group, (g + 1) * per_group):
                blocks.append(meta[b % 2, b // 2])
            flipped = jnp.concatenate(blocks, axis=0).T
            logits_out[:, g * GROUP : (g + 1) * GROUP] = flipped[:experts]
            marks_out[:, g * GROUP : (g + 1) * GROUP] = flipped[experts:]
        kernels_out[0] = jnp.exp(logits_out[...])
        for s in range(ITERS):
            kernel = kernels_out[s]
            column = jnp.sum(kernel, axis=1, keepdims=True)
            scaled = kernel / column
            row = jnp.sum(scaled, axis=0, keepdims=True)
            kernels_out[s + 1] = scaled / row
            columns_out[s] = jnp.broadcast_to(column, (experts, LANES))
            totals_out[s : s + 1, :] = row
        member = marks_out[...] > 0.0
        picked = jnp.where(member, kernels_out[ITERS], 0.0)
        picked_sum = jnp.sum(picked, axis=0, keepdims=True)
        totals_out[ITERS : ITERS + 1, :] = picked_sum
        totals_out[ITERS + 1 :, :] = jnp.broadcast_to(
            jnp.max(marks_out[...], axis=0, keepdims=True),
            (totals_out.shape[0] - ITERS - 1, totals_out.shape[1]),
        )
        own = marks_out[pl.ds(me, 1), :] > 0.0
        gate = jnp.where(own, kernels_out[ITERS, pl.ds(me, 1), :], 0.0) / picked_sum
        row_mask[...] = own.astype(f32)
        row_gate[...] = gate.astype(bf16).astype(f32)

    first, second = len(steps) // 12, len(steps) // 6
    third, fourth = len(steps) // 4, len(steps) // 3
    y_copies, mate_copy = [], None
    for at, step in enumerate(steps):
        if at == first:
            for k, copy in enumerate(z_copies):
                block = y * nz + lax.rem(z - 1 - k + nz, nz)
                meta_copy(k, meta_part(core, block, 1), mate).wait_recv()
            y_copies = [
                meta_copy(nz - 1 + k, meta_part(core, y * nz, nz), p) for k, p in enumerate(y_peers)
            ]
            for copy in y_copies:
                copy.start()
        if at == second:
            for k in range(ny - 1):
                block = lax.rem(y - 1 - k + ny, ny) * nz
                meta_copy(nz - 1 + k, meta_part(core, block, nz), mate).wait_recv()
            mate_copy = meta_copy(nz + ny - 2, meta_part(core, 0, ny * nz), mate)
            mate_copy.start()
        if at == third:
            meta_copy(nz + ny - 2, meta_part(1 - core, 0, ny * nz), mate).wait_recv()
        if at == fourth:
            balance()
        run(step)
    for n, which, dy, dz, part in mate_arrivals:
        block_copy(n, view(which, dy, dz, part, 1 - core), ("mate", 0)).wait_recv()

    before = lax.broadcasted_iota(jnp.int32, (GROUP, GROUP), 0)
    after = lax.broadcasted_iota(jnp.int32, (GROUP, GROUP), 1)
    earlier = jnp.where((before < after) & (before // count == after // count), 1.0, 0.0).astype(bf16)
    slots = per_group * SLOTS
    slot_ids = lax.broadcasted_iota(jnp.int32, (slots, GROUP), 0).astype(f32)
    base = (lax.broadcasted_iota(jnp.int32, (1, GROUP), 1) // count * SLOTS).astype(f32)

    def compact(g, carry):
        lanes = pl.ds(pl.multiple_of(g * GROUP, GROUP), GROUP)
        rows = pl.ds(pl.multiple_of(g * slots, slots), slots)
        named = row_mask[:, lanes]
        rank = jnp.dot(
            jnp.broadcast_to(named, (8, GROUP)).astype(bf16), earlier, preferred_element_type=f32
        )[0:1]
        target = jnp.where(named > 0.0, base + rank, -1.0)
        chosen = jnp.where(slot_ids == target, 1.0, 0.0)
        rows_gate[rows, :] = jnp.sum(chosen * row_gate[:, lanes], axis=1, keepdims=True)
        pick = chosen.astype(bf16)
        pick_out[g] = pick
        blocks = pl.ds(g * per_group, per_group)
        rows_tok[rows, :] = jnp.dot(
            pick, tok_all[blocks].reshape(GROUP, width), preferred_element_type=f32
        ).astype(bf16)
        rows_cot[rows, :] = jnp.dot(
            pick, cot_all[blocks].reshape(GROUP, width), preferred_element_type=f32
        ).astype(bf16)
        return carry

    lax.fori_loop(0, groups, compact, 0)
    share = me // (ep // (width // LANES))
    slice_out[...] = tok_all[:, :, pl.ds(pl.multiple_of(share * LANES, LANES), LANES)]

    for copy in [*z_copies, *y_copies, mate_copy, *started]:
        copy.wait_send()


def dispatch(tokens, cotangent, assign, router, ep):
    ny, nz = torus_of(ep)
    count, width = tokens.shape
    experts = router.shape[1]
    total = ep * count
    groups = total // GROUP
    copies = gather_plan(ny, nz)[1]
    small = nz + ny - 1
    shape = jax.ShapeDtypeStruct
    vmem = pl.BlockSpec(memory_space=pltpu.VMEM)
    return pl.pallas_call(
        functools.partial(dispatch_kernel, ep),
        out_shape=(
            shape((ep * SLOTS, width), bf16),
            shape((ep * SLOTS, width), bf16),
            shape((ep * SLOTS, 1), f32),
            shape((groups, GROUP // count * SLOTS, GROUP), bf16),
            shape((ITERS + 1, experts, total), f32),
            shape((ITERS, experts, LANES), f32),
            shape((8, total), f32),
            shape((experts, total), f32),
            shape((experts, total), f32),
            shape((ep, count, LANES), bf16),
        ),
        in_specs=[vmem] * 4,
        out_specs=(vmem,) * 10,
        scratch_shapes=[
            pltpu.VMEM((ep, count, width), bf16),
            pltpu.VMEM((ep, count, width), bf16),
            pltpu.VMEM((2, ny * nz, count, 2 * experts), f32),
            pltpu.VMEM((1, total), f32),
            pltpu.VMEM((1, total), f32),
            pltpu.SemaphoreType.DMA((small,)),
            pltpu.SemaphoreType.DMA((small,)),
            pltpu.SemaphoreType.DMA((copies,)),
            pltpu.SemaphoreType.DMA((copies,)),
        ],
        compiler_params=pltpu.CompilerParams(
            collective_id=1, has_side_effects=True, vmem_limit_bytes=48 * 2**20
        ),
    )(tokens, cotangent, assign, router)


def split_three(value):
    high = value.astype(bf16)
    rest = value - high.astype(f32)
    middle = rest.astype(bf16)
    return high, middle, (rest - middle.astype(f32)).astype(bf16)


def router_kernel(
    ep,
    n_dp,
    grad_ref,
    pick_ref,
    kernels,
    columns,
    totals,
    logits_ref,
    marks_ref,
    slice_ref,
    tok_ref,
    router_ref,
    back_out,
    router_out,
    table,
    grad,
    spread,
    turned,
    parts,
    shares,
    sends,
    recvs,
):
    ny, nz = torus_of(ep)
    count, width = tok_ref.shape
    experts = router_ref.shape[1]
    total = ep * count
    groups = total // GROUP
    n_shares = width // LANES
    repeat = ep // n_shares
    dp = lax.axis_index("dp")
    me, core, y, z = place(ep, ny, nz)
    mate = (dp, at_ep(nz, y, z, 1 - core))
    z_peers = [(dp, at_ep(nz, y, lax.rem(z + k, nz), core)) for k in range(1, nz)]
    y_peers = [(dp, at_ep(nz, lax.rem(y + k, ny), z, core)) for k in range(1, ny)]
    x_peers = [(lax.rem(dp + k, n_dp), me) for k in range(1, n_dp)]
    share, twin = me // repeat, lax.rem(me, repeat)
    share_peers = [
        (dp, lax.rem(share + k, n_shares) * repeat + twin) for k in range(1, n_shares)
    ]
    enter([mate, *z_peers, *y_peers, *x_peers, *share_peers])

    def copy_of(n, ref, peer):
        return pltpu.make_async_remote_copy(
            src_ref=ref, dst_ref=ref, send_sem=sends.at[n], recv_sem=recvs.at[n],
            device_id=peer, device_id_type=MESH,
        )

    mine = y * nz + z
    for g in range(groups):
        row = jnp.dot(
            grad_ref[:, g * GROUP // count * SLOTS : (g + 1) * GROUP // count * SLOTS],
            pick_ref[g],
            preferred_element_type=f32,
        )
        table[mine, core, g : g + 1, :] = row[0:1]
    n = 0
    all_copies = []

    def part(chip, chips):
        return table.at[pl.ds(chip, chips)]

    copy = copy_of(n, table.at[mine, core], mate)
    copy.start()
    all_copies.append(copy)
    copy_of(n, table.at[mine, 1 - core], mate).wait_recv()
    n += 1
    for k, peer in enumerate(z_peers):
        copy = copy_of(n + k, part(mine, 1), peer)
        copy.start()
        all_copies.append(copy)
    for k in range(nz - 1):
        copy_of(n + k, part(y * nz + lax.rem(z - 1 - k + nz, nz), 1), mate).wait_recv()
    n += nz - 1
    for k, peer in enumerate(y_peers):
        copy = copy_of(n + k, part(y * nz, nz), peer)
        copy.start()
        all_copies.append(copy)
    for k in range(ny - 1):
        copy_of(n + k, part(lax.rem(y - 1 - k + ny, ny) * nz, nz), mate).wait_recv()
    n += ny - 1

    for g in range(groups):
        both = table[:, :, g, :]
        grad[:, g * GROUP : (g + 1) * GROUP] = both.reshape(experts, GROUP)
    inverse_token = totals[ITERS + 1 : ITERS + 2, :]
    picked_sum = totals[ITERS : ITERS + 1, :]
    member = marks_ref[...] > 0.0
    route = jnp.where(member, grad[...], 0.0)
    gates = jnp.where(member, kernels[ITERS], 0.0) / picked_sum
    grad[...] = jnp.where(
        member, (route - jnp.sum(route * gates, axis=0, keepdims=True)) / picked_sum, 0.0
    )
    for s in reversed(range(ITERS)):
        kernel = kernels[s + 1]
        row = totals[s : s + 1, :]
        column = columns[s][:, 0:1]
        slope = grad[...]
        slope = (slope - jnp.sum(slope * kernel, axis=0, keepdims=True)) / row
        moment = jnp.sum(slope * (kernel * row), axis=1, keepdims=True)
        grad[...] = (slope - moment) / column
    logit_grad = grad[...] * kernels[0]
    weighted = logit_grad * logits_ref[...]
    router = router_ref[...]
    router_wide = router.astype(f32)
    square = jnp.sum(router_wide * router_wide, axis=0, keepdims=True) + eps_norm
    square = jnp.broadcast_to(square, (LANES, experts)).T[:, 0:1]
    turn = logit_grad * (cos_scale * inverse_token) / jnp.sqrt(square)
    spread[:experts, :] = turn
    spread[experts:, :] = jnp.broadcast_to(
        jnp.sum(weighted, axis=0, keepdims=True) * inverse_token * inverse_token,
        (spread.shape[0] - experts, total),
    )

    features = slice_ref[...].reshape(total, LANES)
    product = jnp.dot(
        jnp.concatenate(split_three(turn), axis=0), features, preferred_element_type=f32
    )
    product = product[:experts] + product[experts : 2 * experts] + product[2 * experts :]
    own_router = router_ref[pl.ds(pl.multiple_of(share * LANES, LANES), LANES), :].astype(f32).T
    parts[dp] = product - own_router * (jnp.sum(weighted, axis=1, keepdims=True) / square)
    for k, peer in enumerate(x_peers):
        copy = copy_of(n + k, parts.at[dp], peer)
        copy.start()
        all_copies.append(copy)

    turned[...] = spread[:, pl.ds(pl.multiple_of(me * count // LANES * LANES, LANES), LANES)].T
    own = turned[pl.ds(pl.multiple_of(lax.rem(me, LANES // count) * count, count), count), :]
    back = jnp.zeros((count, width), f32)
    for term in split_three(own[:, :experts]):
        back += lax.dot_general(term, router, contract_last, preferred_element_type=f32)
    back_out[...] = back - tok_ref[...].astype(f32) * own[:, experts : experts + 1]

    for k in range(n_dp - 1):
        copy_of(n + k, parts.at[lax.rem(dp - 1 - k + n_dp, n_dp)], mate).wait_recv()
    n += n_dp - 1
    summed = parts[0]
    for k in range(1, n_dp):
        summed += parts[k]
    shares[share] = summed
    for k, peer in enumerate(share_peers):
        copy = copy_of(n + k, shares.at[share], peer)
        copy.start()
        all_copies.append(copy)
    for k in range(n_shares - 1):
        copy_of(n + k, shares.at[lax.rem(share - 1 - k + n_shares, n_shares)], mate).wait_recv()
    for k in range(n_shares):
        router_out[k * LANES : (k + 1) * LANES, :] = shares[k].T
    for copy in all_copies:
        copy.wait_send()


def router_backward(gate_grad, pick, saved, features, tokens, router, ep, n_dp):
    ny, nz = torus_of(ep)
    kernels, columns, totals, logits, marks = saved
    count, width = tokens.shape
    experts = router.shape[1]
    total = ep * count
    n_shares = width // LANES
    copies = 1 + nz - 1 + ny - 1 + n_dp - 1 + n_shares - 1
    vmem = pl.BlockSpec(memory_space=pltpu.VMEM)
    return pl.pallas_call(
        functools.partial(router_kernel, ep, n_dp),
        out_shape=(
            jax.ShapeDtypeStruct((count, width), f32),
            jax.ShapeDtypeStruct((width, experts), f32),
        ),
        in_specs=[vmem] * 10,
        out_specs=(vmem, vmem),
        scratch_shapes=[
            pltpu.VMEM((ny * nz, 2, total // GROUP, GROUP), f32),
            pltpu.VMEM((experts, total), f32),
            pltpu.VMEM((LANES, total), f32),
            pltpu.VMEM((LANES, LANES), f32),
            pltpu.VMEM((n_dp, experts, LANES), f32),
            pltpu.VMEM((n_shares, experts, LANES), f32),
            pltpu.SemaphoreType.DMA((copies,)),
            pltpu.SemaphoreType.DMA((copies,)),
        ],
        compiler_params=pltpu.CompilerParams(
            collective_id=2, has_side_effects=True, vmem_limit_bytes=40 * 2**20
        ),
    )(
        jnp.broadcast_to(gate_grad[None, :], (8, gate_grad.shape[0])),
        pick,
        kernels,
        columns,
        totals,
        logits,
        marks,
        features,
        tokens,
        router,
    )


def per_device(ep, n_dp, tokens, cotangent, assign, w_router, w_gate, w_up, w_down):
    local_tokens = tokens[0]
    count, width = local_tokens.shape
    experts = w_router.shape[1]
    rows, cotangent_rows, rows_gate, pick, kernels, columns, totals, logits, marks, features = dispatch(
        local_tokens, cotangent[0], assign[0], w_router, ep
    )
    gate_matrix, up_matrix, down_matrix = w_gate[0], w_up[0], w_down[0]

    def reduced(left, right):
        product = lax.dot_general(left, right, contract_first, preferred_element_type=f32)
        return lax.psum_scatter(
            product.astype(bf16), "dp", scatter_dimension=0, tiled=True
        )[None]

    gate_linear = jnp.dot(rows, gate_matrix, preferred_element_type=f32)
    up_linear = jnp.dot(rows, up_matrix, preferred_element_type=f32)
    sigmoid_gate = jax.nn.sigmoid(gate_linear)
    activation = gate_linear * sigmoid_gate
    product = activation * up_linear
    hidden = product.astype(bf16)
    weighted = (rows_gate * product).astype(bf16)
    grad_down = reduced(cotangent_rows, weighted)
    raw_back = jnp.dot(cotangent_rows, down_matrix, preferred_element_type=f32)
    gate_grad = jnp.sum(raw_back * hidden.astype(f32), axis=1).astype(bf16)
    scaled_back = rows_gate * raw_back
    up_delta = (scaled_back * activation).astype(bf16)
    gate_delta = (
        scaled_back * up_linear * sigmoid_gate * (1.0 + gate_linear * (1.0 - sigmoid_gate))
    ).astype(bf16)
    grad_up = reduced(rows, up_delta)
    grad_gate = reduced(rows, gate_delta)
    route_back = (
        lax.dot_general(gate_delta, gate_matrix, contract_last, preferred_element_type=f32)
        + lax.dot_general(up_delta, up_matrix, contract_last, preferred_element_type=f32)
    ).astype(bf16)
    back_rows = lax.all_to_all(
        route_back.reshape(ep, SLOTS, width), "ep", split_axis=0, concat_axis=0, tiled=True
    )
    router_back, grad_router = router_backward(
        gate_grad, pick, (kernels, columns, totals, logits, marks), features, local_tokens, w_router, ep, n_dp
    )

    named = jnp.any(
        assign[0][:, :, None] == jnp.arange(experts, dtype=jnp.int32), axis=1
    ).astype(bf16)
    order = jnp.arange(count)
    earlier = (order[:, None] > order[None, :]).astype(bf16)
    rank = jnp.dot(earlier, named, preferred_element_type=f32)
    slot_of = jnp.where(named > 0, rank, -1.0)
    token_slots = (
        slot_of[:, :, None] == jnp.arange(SLOTS, dtype=f32)
    ).astype(bf16).reshape(count, experts * SLOTS)
    expert_back = jnp.dot(token_slots, back_rows.reshape(-1, width), preferred_element_type=f32)
    grad_tokens = (expert_back + router_back).astype(bf16)[None]
    return grad_tokens, grad_router, grad_gate, grad_up, grad_down


def solution(mesh):
    return jax.shard_map(
        functools.partial(per_device, mesh.shape["ep"], mesh.shape["dp"]),
        mesh=mesh,
        in_specs=(
            P("dp", "ep", None),
            P("dp", "ep", None),
            P("dp", "ep", None),
            P(),
            P("ep", None, None),
            P("ep", None, None),
            P("ep", None, None),
        ),
        out_specs=(
            P("dp", "ep", None),
            P(),
            P("ep", "dp", None),
            P("ep", "dp", None),
            P("ep", "dp", None),
        ),
        check_vma=False,
    )
```

```python
import functools
import heapq

import jax
import jax.numpy as jnp
from jax import lax
from jax.experimental import pallas as pl
from jax.experimental.pallas import tpu as pltpu
from jax.sharding import PartitionSpec as P

ITERS = 3
SLOTS = 8
LANES = 128
GROUP = 256
MESH = pl.DeviceIdType.MESH
f32 = jnp.float32
bf16 = jnp.bfloat16

cos_scale = 48.0
eps_norm = 1e-06
contract_first = (((0,), (0,)), ((), ()))
contract_last = (((1,), (1,)), ((), ()))


def torus_of(ep):
    ny = max(1, min(4, ep // 4))
    return ny, ep // (2 * ny)


def gather_plan(ny, nz, unit_us=2.7, mate_us=0.5, hop_us=1.0):
    def half(part, side):
        return side if part is None else (part if part == side else -1)

    def spread(which, a, b, part):
        na, nb = (nz, ny) if which == 0 else (ny, nz)
        out = []

        def along(axis, n, at, signs):
            for sign in signs:
                last = abs(at) + 1 == n // 2
                piece = half(part, 0 if sign > 0 else 1) if last else part
                if piece != -1:
                    out.append((axis, sign, piece))

        def onward(at, n):
            if n == 1:
                return ()
            if at == 0:
                return (1, -1)
            return ((1,) if at > 0 else (-1,)) if abs(at) < n // 2 else ()

        if b == 0:
            along(0, na, a, onward(a, na))
        along(1, nb, b, onward(b, nb))
        return out

    heap, order, free, steps, ids = [], 0, {}, [], 0
    for which in (0, 1):
        heapq.heappush(heap, (0.0, order, None, which, 0, 0, None))
        order += 1
    while heap:
        now, _, arrival, which, a, b, part = heapq.heappop(heap)
        dy, dz = (b, a) if which == 0 else (a, b)
        sends = []
        for axis, sign, piece in spread(which, a, b, part):
            link = "zy"[axis] if which == 0 else "yz"[axis]
            share = 1.0 if piece is None else 0.5
            end = max(now, free.get((link, sign), 0.0)) + unit_us * share
            free[(link, sign)] = end
            na, nb = (a + sign, b) if axis == 0 else (a, b + sign)
            heapq.heappush(heap, (end + hop_us, order, ids, which, na, nb, piece))
            sends.append((ids, which, dy, dz, part if piece is None else piece, link, sign))
            order += 1
            ids += 1
        sends.append((ids, which, dy, dz, part, "mate", 0))
        ids += 1
        steps.append((None if arrival is None else (arrival, which, dy, dz, part), sends))
    return steps, ids


def place(ep, ny, nz):
    me = lax.axis_index("ep")
    core = lax.rem(me, 2)
    chip = me // 2
    return me, core, chip // nz, lax.rem(chip, nz)


def at_ep(nz, y, z, core):
    return (y * nz + z) * 2 + core


def enter(peers):
    barrier = pltpu.get_barrier_semaphore()
    for peer in peers:
        pl.semaphore_signal(barrier, inc=1, device_id=peer, device_id_type=MESH)
    pl.semaphore_wait(barrier, len(peers))


def dispatch_kernel(
    ep,
    tok_ref,
    cot_ref,
    assign_ref,
    router_ref,
    rows_tok,
    rows_cot,
    rows_gate,
    pick_out,
    kernels_out,
    columns_out,
    totals_out,
    logits_out,
    marks_out,
    slice_out,
    tok_all,
    cot_all,
    meta,
    row_mask,
    row_gate,
    meta_send,
    meta_recv,
    send_sem,
    recv_sem,
):
    ny, nz = torus_of(ep)
    count, width = tok_ref.shape
    experts = router_ref.shape[1]
    groups = ep * count // GROUP
    per_group = GROUP // count
    dp = lax.axis_index("dp")
    me, core, y, z = place(ep, ny, nz)
    mate = (dp, at_ep(nz, y, z, 1 - core))
    z_peers = [(dp, at_ep(nz, y, lax.rem(z + k, nz), core)) for k in range(1, nz)]
    y_peers = [(dp, at_ep(nz, lax.rem(y + k, ny), z, core)) for k in range(1, ny)]
    enter([mate, *z_peers, *y_peers])

    local = tok_ref[...]
    router = router_ref[...]
    wide = local.astype(f32)
    inverse_token = 1.0 / jnp.sqrt(jnp.sum(wide * wide, axis=1, keepdims=True) + eps_norm)
    router_wide = router.astype(f32)
    column_norm = jnp.sqrt(jnp.sum(router_wide * router_wide, axis=0, keepdims=True) + eps_norm)
    inner = jnp.dot(local, router, preferred_element_type=f32)
    logits = cos_scale * inner * inverse_token / column_norm
    ids = lax.broadcasted_iota(jnp.int32, (count, experts), 1)
    routes = assign_ref[...]
    hit = jnp.zeros((count, experts), f32)
    for k in range(routes.shape[1]):
        hit = jnp.where(routes[:, k : k + 1] == ids, inverse_token, hit)
    mine = y * nz + z
    meta[core, mine] = jnp.concatenate([logits, hit], axis=1)
    tok_all[me] = local
    cot_all[me] = cot_ref[...]

    def meta_copy(n, part, peer):
        return pltpu.make_async_remote_copy(
            src_ref=part, dst_ref=part, send_sem=meta_send.at[n], recv_sem=meta_recv.at[n],
            device_id=peer, device_id_type=MESH,
        )

    def meta_part(c, block, blocks):
        return meta.at[c, pl.ds(block, blocks)]

    z_copies = [meta_copy(k, meta_part(core, mine, 1), p) for k, p in enumerate(z_peers)]
    for copy in z_copies:
        copy.start()

    steps, total = gather_plan(ny, nz)
    ends = {
        ("z", 1): (dp, at_ep(nz, y, lax.rem(z + 1, nz), core)),
        ("z", -1): (dp, at_ep(nz, y, lax.rem(z + nz - 1, nz), core)),
        ("y", 1): (dp, at_ep(nz, lax.rem(y + 1, ny), z, core)),
        ("y", -1): (dp, at_ep(nz, lax.rem(y + ny - 1, ny), z, core)),
        ("mate", 0): mate,
    }
    tables = (tok_all, cot_all)

    def view(which, dy, dz, part, c):
        block = at_ep(nz, lax.rem(y - dy + 2 * ny, ny), lax.rem(z - dz + 2 * nz, nz), c)
        first, rows = (0, count) if part is None else (part * (count // 2), count // 2)
        return tables[which].at[block, pl.ds(first, rows)]

    def block_copy(n, ref, end):
        return pltpu.make_async_remote_copy(
            src_ref=ref, dst_ref=ref, send_sem=send_sem.at[n], recv_sem=recv_sem.at[n],
            device_id=ends[end], device_id_type=MESH,
        )

    started, mate_arrivals = [], []

    def run(step):
        arrival, sends = step
        if arrival is not None:
            n, which, dy, dz, part = arrival
            block_copy(n, view(which, dy, dz, part, core), ("z", 1)).wait_recv()
        for n, which, dy, dz, part, link, sign in sends:
            copy = block_copy(n, view(which, dy, dz, part, core), (link, sign))
            copy.start()
            started.append(copy)
            if link == "mate":
                mate_arrivals.append((n, which, dy, dz, part))

    def balance():
        for g in range(groups):
            blocks = []
            for b in range(g * per_group, (g + 1) * per_group):
                blocks.append(meta[b % 2, b // 2])
            flipped = jnp.concatenate(blocks, axis=0).T
            logits_out[:, g * GROUP : (g + 1) * GROUP] = flipped[:experts]
            marks_out[:, g * GROUP : (g + 1) * GROUP] = flipped[experts:]
        kernels_out[0] = jnp.exp(logits_out[...])
        for s in range(ITERS):
            kernel = kernels_out[s]
            column = jnp.sum(kernel, axis=1, keepdims=True)
            scaled = kernel / column
            row = jnp.sum(scaled, axis=0, keepdims=True)
            kernels_out[s + 1] = scaled / row
            columns_out[s] = jnp.broadcast_to(column, (experts, LANES))
            totals_out[s : s + 1, :] = row
        member = marks_out[...] > 0.0
        picked = jnp.where(member, kernels_out[ITERS], 0.0)
        picked_sum = jnp.sum(picked, axis=0, keepdims=True)
        totals_out[ITERS : ITERS + 1, :] = picked_sum
        totals_out[ITERS + 1 :, :] = jnp.broadcast_to(
            jnp.max(marks_out[...], axis=0, keepdims=True),
            (totals_out.shape[0] - ITERS - 1, totals_out.shape[1]),
        )
        own = marks_out[pl.ds(me, 1), :] > 0.0
        gate = jnp.where(own, kernels_out[ITERS, pl.ds(me, 1), :], 0.0) / picked_sum
        row_mask[...] = own.astype(f32)
        row_gate[...] = gate.astype(bf16).astype(f32)

    first, second = len(steps) // 12, len(steps) // 6
    third, fourth = len(steps) // 4, len(steps) // 3
    y_copies, mate_copy = [], None
    for at, step in enumerate(steps):
        if at == first:
            for k, copy in enumerate(z_copies):
                block = y * nz + lax.rem(z - 1 - k + nz, nz)
                meta_copy(k, meta_part(core, block, 1), mate).wait_recv()
            y_copies = [
                meta_copy(nz - 1 + k, meta_part(core, y * nz, nz), p) for k, p in enumerate(y_peers)
            ]
            for copy in y_copies:
                copy.start()
        if at == second:
            for k in range(ny - 1):
                block = lax.rem(y - 1 - k + ny, ny) * nz
                meta_copy(nz - 1 + k, meta_part(core, block, nz), mate).wait_recv()
            mate_copy = meta_copy(nz + ny - 2, meta_part(core, 0, ny * nz), mate)
            mate_copy.start()
        if at == third:
            meta_copy(nz + ny - 2, meta_part(1 - core, 0, ny * nz), mate).wait_recv()
        if at == fourth:
            balance()
        run(step)
    for n, which, dy, dz, part in mate_arrivals:
        block_copy(n, view(which, dy, dz, part, 1 - core), ("mate", 0)).wait_recv()

    before = lax.broadcasted_iota(jnp.int32, (GROUP, GROUP), 0)
    after = lax.broadcasted_iota(jnp.int32, (GROUP, GROUP), 1)
    earlier = jnp.where((before < after) & (before // count == after // count), 1.0, 0.0).astype(bf16)
    slots = per_group * SLOTS
    slot_ids = lax.broadcasted_iota(jnp.int32, (slots, GROUP), 0).astype(f32)
    base = (lax.broadcasted_iota(jnp.int32, (1, GROUP), 1) // count * SLOTS).astype(f32)

    def compact(g, carry):
        lanes = pl.ds(pl.multiple_of(g * GROUP, GROUP), GROUP)
        rows = pl.ds(pl.multiple_of(g * slots, slots), slots)
        named = row_mask[:, lanes]
        rank = jnp.dot(
            jnp.broadcast_to(named, (8, GROUP)).astype(bf16), earlier, preferred_element_type=f32
        )[0:1]
        target = jnp.where(named > 0.0, base + rank, -1.0)
        chosen = jnp.where(slot_ids == target, 1.0, 0.0)
        rows_gate[rows, :] = jnp.sum(chosen * row_gate[:, lanes], axis=1, keepdims=True)
        pick = chosen.astype(bf16)
        pick_out[g] = pick
        blocks = pl.ds(g * per_group, per_group)
        rows_tok[rows, :] = jnp.dot(
            pick, tok_all[blocks].reshape(GROUP, width), preferred_element_type=f32
        ).astype(bf16)
        rows_cot[rows, :] = jnp.dot(
            pick, cot_all[blocks].reshape(GROUP, width), preferred_element_type=f32
        ).astype(bf16)
        return carry

    lax.fori_loop(0, groups, compact, 0)
    share = me // (ep // (width // LANES))
    slice_out[...] = tok_all[:, :, pl.ds(pl.multiple_of(share * LANES, LANES), LANES)]

    for copy in [*z_copies, *y_copies, mate_copy, *started]:
        copy.wait_send()


def dispatch(tokens, cotangent, assign, router, ep):
    ny, nz = torus_of(ep)
    count, width = tokens.shape
    experts = router.shape[1]
    total = ep * count
    groups = total // GROUP
    copies = gather_plan(ny, nz)[1]
    small = nz + ny - 1
    shape = jax.ShapeDtypeStruct
    vmem = pl.BlockSpec(memory_space=pltpu.VMEM)
    return pl.pallas_call(
        functools.partial(dispatch_kernel, ep),
        out_shape=(
            shape((ep * SLOTS, width), bf16),
            shape((ep * SLOTS, width), bf16),
            shape((ep * SLOTS, 1), f32),
            shape((groups, GROUP // count * SLOTS, GROUP), bf16),
            shape((ITERS + 1, experts, total), f32),
            shape((ITERS, experts, LANES), f32),
            shape((8, total), f32),
            shape((experts, total), f32),
            shape((experts, total), f32),
            shape((ep, count, LANES), bf16),
        ),
        in_specs=[vmem] * 4,
        out_specs=(vmem,) * 10,
        scratch_shapes=[
            pltpu.VMEM((ep, count, width), bf16),
            pltpu.VMEM((ep, count, width), bf16),
            pltpu.VMEM((2, ny * nz, count, 2 * experts), f32),
            pltpu.VMEM((1, total), f32),
            pltpu.VMEM((1, total), f32),
            pltpu.SemaphoreType.DMA((small,)),
            pltpu.SemaphoreType.DMA((small,)),
            pltpu.SemaphoreType.DMA((copies,)),
            pltpu.SemaphoreType.DMA((copies,)),
        ],
        compiler_params=pltpu.CompilerParams(
            collective_id=1, has_side_effects=True, vmem_limit_bytes=48 * 2**20
        ),
    )(tokens, cotangent, assign, router)


def split_three(value):
    high = value.astype(bf16)
    rest = value - high.astype(f32)
    middle = rest.astype(bf16)
    return high, middle, (rest - middle.astype(f32)).astype(bf16)


def backward_kernel(
    ep,
    n_dp,
    grad_ref,
    pick_ref,
    kernels,
    columns,
    totals,
    logits_ref,
    marks_ref,
    slice_ref,
    tok_ref,
    router_ref,
    rows_ref,
    cot_rows_ref,
    gate_delta,
    up_delta,
    weighted_ref,
    slots_ref,
    w_gate_hbm,
    w_up_hbm,
    tokens_out,
    router_out,
    gate_out,
    up_out,
    down_out,
    w_gate,
    w_up,
    table,
    grad,
    spread,
    turned,
    parts,
    shares,
    route_back,
    back_rows,
    sent_far,
    got_far,
    sent_near,
    got_near,
    own_sum,
    sends,
    recvs,
    row_sends,
    row_recvs,
    far_sends,
    far_recvs,
    near_sends,
    near_recvs,
    weight_sems,
):
    ny, nz = torus_of(ep)
    count, width = tok_ref.shape
    experts = router_ref.shape[1]
    total = ep * count
    groups = total // GROUP
    n_shares = width // LANES
    repeat = ep // n_shares
    chunk = width // n_dp // 2
    dp = lax.axis_index("dp")
    me, core, y, z = place(ep, ny, nz)
    mate = (dp, at_ep(nz, y, z, 1 - core))
    z_peers = [(dp, at_ep(nz, y, lax.rem(z + k, nz), core)) for k in range(1, nz)]
    y_peers = [(dp, at_ep(nz, lax.rem(y + k, ny), z, core)) for k in range(1, ny)]
    x_peers = [(lax.rem(dp + k, n_dp), me) for k in range(1, n_dp)]
    right, left = (lax.rem(dp + 1, n_dp), me), (lax.rem(dp + n_dp - 1, n_dp), me)
    share, twin = me // repeat, lax.rem(me, repeat)
    share_peers = [
        (dp, lax.rem(share + k, n_shares) * repeat + twin) for k in range(1, n_shares)
    ]

    fetch_gate = pltpu.make_async_copy(w_gate_hbm, w_gate, weight_sems.at[0])
    fetch_up = pltpu.make_async_copy(w_up_hbm, w_up, weight_sems.at[1])
    fetch_gate.start()
    fetch_up.start()

    barrier = pltpu.get_barrier_semaphore()

    def greet(k, carry):
        pl.semaphore_signal(
            barrier, inc=1, device_id=(dp, lax.rem(me + k, ep)), device_id_type=MESH
        )
        return carry

    lax.fori_loop(1, ep, greet, 0)
    for peer in x_peers:
        pl.semaphore_signal(barrier, inc=1, device_id=peer, device_id_type=MESH)
    pl.semaphore_wait(barrier, ep - 1 + n_dp - 1)

    started = []

    def copy_of(n, ref, peer):
        return pltpu.make_async_remote_copy(
            src_ref=ref, dst_ref=ref, send_sem=sends.at[n], recv_sem=recvs.at[n],
            device_id=peer, device_id_type=MESH,
        )

    def start(copy):
        copy.start()
        started.append(copy)

    def far_copy(a, side):
        return pltpu.make_async_remote_copy(
            src_ref=sent_far.at[a, side], dst_ref=got_far.at[a, side],
            send_sem=far_sends.at[a, side], recv_sem=far_recvs.at[a, side],
            device_id=(right, left)[side], device_id_type=MESH,
        )

    def near_copy(a, side, half):
        return pltpu.make_async_remote_copy(
            src_ref=sent_near.at[a, side, half], dst_ref=got_near.at[a, side, half],
            send_sem=near_sends.at[a, side, half], recv_sem=near_recvs.at[a, side, half],
            device_id=(right, left)[side], device_id_type=MESH,
        )

    pairs = ((cot_rows_ref, weighted_ref), (rows_ref, up_delta), (rows_ref, gate_delta))
    outs = (down_out, up_out, gate_out)
    arrays = range(3)

    def gradient(a, away, half):
        block = lax.rem(dp + away, n_dp)
        first = pl.multiple_of(block * (2 * chunk) + half * chunk, chunk)
        left_rows, right_rows = pairs[a]
        return lax.dot_general(
            left_rows[:, pl.ds(first, chunk)], right_rows[...], contract_first,
            preferred_element_type=f32,
        )

    mine = y * nz + z
    for g in range(groups):
        row = jnp.dot(
            grad_ref[:, g * GROUP // count * SLOTS : (g + 1) * GROUP // count * SLOTS],
            pick_ref[g],
            preferred_element_type=f32,
        )
        table[mine, core, g : g + 1, :] = row[0:1]
    n = 0

    def part(chip, chips):
        return table.at[pl.ds(chip, chips)]

    start(copy_of(n, table.at[mine, core], mate))

    def far(a):
        for side in range(2):
            sent_far[a, side] = gradient(a, 2, side).astype(bf16)
            start(far_copy(a, side))

    def near_plain(a):
        for side in range(2):
            sent_near[a, side, 1 - side] = gradient(a, (1, n_dp - 1)[side], 1 - side).astype(bf16)
            start(near_copy(a, side, 1 - side))

    def near_joined(a):
        for side in range(2):
            mixed = gradient(a, (1, n_dp - 1)[side], side)
            far_copy(a, side).wait_recv()
            sent_near[a, side, side] = (mixed + got_far[a, side].astype(f32)).astype(bf16)
            start(near_copy(a, side, side))

    ring = n_dp == 4
    if ring:
        far(0)
    copy_of(n, table.at[mine, 1 - core], mate).wait_recv()
    n += 1
    for k, peer in enumerate(z_peers):
        start(copy_of(n + k, part(mine, 1), peer))
    if ring:
        far(1)
        far(2)
    for k in range(nz - 1):
        copy_of(n + k, part(y * nz + lax.rem(z - 1 - k + nz, nz), 1), mate).wait_recv()
    n += nz - 1
    for k, peer in enumerate(y_peers):
        start(copy_of(n + k, part(y * nz, nz), peer))

    fetch_gate.wait()
    fetch_up.wait()
    pieces = 4
    rows_each = ep // pieces

    def rows_back(q, carry):
        rows = pl.ds(pl.multiple_of(q * rows_each * SLOTS, rows_each * SLOTS), rows_each * SLOTS)
        value = lax.dot_general(
            gate_delta[rows, :], w_gate[...], contract_last, preferred_element_type=f32
        ) + lax.dot_general(up_delta[rows, :], w_up[...], contract_last, preferred_element_type=f32)
        route_back[pl.ds(q * rows_each, rows_each)] = value.astype(bf16).reshape(
            rows_each, SLOTS, width
        )
        return carry

    lax.fori_loop(0, pieces, rows_back, 0)

    def row_copy(k, from_block, to_block, peer):
        return pltpu.make_async_remote_copy(
            src_ref=route_back.at[from_block], dst_ref=back_rows.at[to_block],
            send_sem=row_sends.at[k], recv_sem=row_recvs.at[k],
            device_id=(dp, peer), device_id_type=MESH,
        )

    def send_rows(k, carry):
        peer = lax.rem(me + k, ep)
        row_copy(k, peer, me, peer).start()
        return carry

    lax.fori_loop(1, ep, send_rows, 0)
    back_rows[me] = route_back[me]

    for k in range(ny - 1):
        copy_of(n + k, part(lax.rem(y - 1 - k + ny, ny) * nz, nz), mate).wait_recv()
    n += ny - 1

    for g in range(groups):
        both = table[:, :, g, :]
        grad[:, g * GROUP : (g + 1) * GROUP] = both.reshape(experts, GROUP)
    inverse_token = totals[ITERS + 1 : ITERS + 2, :]
    picked_sum = totals[ITERS : ITERS + 1, :]
    member = marks_ref[...] > 0.0
    route = jnp.where(member, grad[...], 0.0)
    gates = jnp.where(member, kernels[ITERS], 0.0) / picked_sum
    grad[...] = jnp.where(
        member, (route - jnp.sum(route * gates, axis=0, keepdims=True)) / picked_sum, 0.0
    )
    for s in reversed(range(ITERS)):
        kernel = kernels[s + 1]
        row = totals[s : s + 1, :]
        column = columns[s][:, 0:1]
        slope = grad[...]
        slope = (slope - jnp.sum(slope * kernel, axis=0, keepdims=True)) / row
        moment = jnp.sum(slope * (kernel * row), axis=1, keepdims=True)
        grad[...] = (slope - moment) / column
    logit_grad = grad[...] * kernels[0]
    weighted = logit_grad * logits_ref[...]
    router = router_ref[...]
    router_wide = router.astype(f32)
    square = jnp.sum(router_wide * router_wide, axis=0, keepdims=True) + eps_norm
    square = jnp.broadcast_to(square, (LANES, experts)).T[:, 0:1]
    turn = logit_grad * (cos_scale * inverse_token) / jnp.sqrt(square)
    spread[:experts, :] = turn
    spread[experts:, :] = jnp.broadcast_to(
        jnp.sum(weighted, axis=0, keepdims=True) * inverse_token * inverse_token,
        (spread.shape[0] - experts, total),
    )

    features = slice_ref[...].reshape(total, LANES)
    product = jnp.dot(
        jnp.concatenate(split_three(turn), axis=0), features, preferred_element_type=f32
    )
    product = product[:experts] + product[experts : 2 * experts] + product[2 * experts :]
    own_router = router_ref[pl.ds(pl.multiple_of(share * LANES, LANES), LANES), :].astype(f32).T
    parts[dp] = product - own_router * (jnp.sum(weighted, axis=1, keepdims=True) / square)
    for k, peer in enumerate(x_peers):
        start(copy_of(n + k, parts.at[dp], peer))

    if ring:
        for a in arrays:
            near_plain(a)
        for a in arrays:
            near_joined(a)

    turned[...] = spread[:, pl.ds(pl.multiple_of(me * count // LANES * LANES, LANES), LANES)].T
    own = turned[pl.ds(pl.multiple_of(lax.rem(me, LANES // count) * count, count), count), :]
    back = jnp.zeros((count, width), f32)
    for term in split_three(own[:, :experts]):
        back += lax.dot_general(term, router, contract_last, preferred_element_type=f32)
    back -= tok_ref[...].astype(f32) * own[:, experts : experts + 1]

    for a in arrays:
        for half in range(2):
            own_sum[a, half] = gradient(a, 0, half)

    for k in range(n_dp - 1):
        copy_of(n + k, parts.at[lax.rem(dp - 1 - k + n_dp, n_dp)], mate).wait_recv()
    n += n_dp - 1
    summed = parts[0]
    for k in range(1, n_dp):
        summed += parts[k]
    shares[share] = summed
    for k, peer in enumerate(share_peers):
        start(copy_of(n + k, shares.at[share], peer))

    def got_rows(k, carry):
        block = lax.rem(me - k + ep, ep)
        row_copy(k, block, block, block).wait_recv()
        return carry

    lax.fori_loop(1, ep, got_rows, 0)
    tokens_out[...] = (
        back
        + jnp.dot(
            slots_ref[...], back_rows[...].reshape(ep * SLOTS, width), preferred_element_type=f32
        )
    ).astype(bf16)

    for k in range(n_shares - 1):
        copy_of(n + k, shares.at[lax.rem(share - 1 - k + n_shares, n_shares)], mate).wait_recv()
    for k in range(n_shares):
        router_out[k * LANES : (k + 1) * LANES, :] = shares[k].T

    def finish(a, half):
        value = own_sum[a, half]
        if ring:
            for side in range(2):
                near_copy(a, side, half).wait_recv()
                value += got_near[a, side, half].astype(f32)
        outs[a][half * chunk : (half + 1) * chunk, :] = value.astype(bf16)

    for a in arrays:
        for half in range(2):
            finish(a, half)

    def sent_rows(k, carry):
        peer = lax.rem(me + k, ep)
        row_copy(k, peer, me, peer).wait_send()
        return carry

    lax.fori_loop(1, ep, sent_rows, 0)
    for copy in started:
        copy.wait_send()


def backward(
    gate_grad, pick, saved, features, tokens, router, rows, cotangent_rows, deltas, slots, weights, ep, n_dp
):
    ny, nz = torus_of(ep)
    kernels, columns, totals, logits, marks = saved
    count, width = tokens.shape
    experts = router.shape[1]
    hidden_units = deltas[0].shape[1]
    total = ep * count
    n_shares = width // LANES
    copies = 1 + nz - 1 + ny - 1 + n_dp - 1 + n_shares - 1
    chunk = width // n_dp // 2
    vmem = pl.BlockSpec(memory_space=pltpu.VMEM)
    anywhere = pl.BlockSpec(memory_space=pl.ANY)
    dma = pltpu.SemaphoreType.DMA
    gradient = jax.ShapeDtypeStruct((2 * chunk, hidden_units), bf16)
    return pl.pallas_call(
        functools.partial(backward_kernel, ep, n_dp),
        out_shape=(
            jax.ShapeDtypeStruct((count, width), bf16),
            jax.ShapeDtypeStruct((width, experts), f32),
            gradient,
            gradient,
            gradient,
        ),
        in_specs=[vmem] * 16 + [anywhere] * 2,
        out_specs=(vmem,) * 5,
        scratch_shapes=[
            pltpu.VMEM((width, hidden_units), bf16),
            pltpu.VMEM((width, hidden_units), bf16),
            pltpu.VMEM((ny * nz, 2, total // GROUP, GROUP), f32),
            pltpu.VMEM((experts, total), f32),
            pltpu.VMEM((LANES, total), f32),
            pltpu.VMEM((LANES, LANES), f32),
            pltpu.VMEM((n_dp, experts, LANES), f32),
            pltpu.VMEM((n_shares, experts, LANES), f32),
            pltpu.VMEM((ep, SLOTS, width), bf16),
            pltpu.VMEM((ep, SLOTS, width), bf16),
            pltpu.VMEM((3, 2, chunk, hidden_units), bf16),
            pltpu.VMEM((3, 2, chunk, hidden_units), bf16),
            pltpu.VMEM((3, 2, 2, chunk, hidden_units), bf16),
            pltpu.VMEM((3, 2, 2, chunk, hidden_units), bf16),
            pltpu.VMEM((3, 2, chunk, hidden_units), f32),
            dma((copies,)),
            dma((copies,)),
            dma((ep,)),
            dma((ep,)),
            dma((3, 2)),
            dma((3, 2)),
            dma((3, 2, 2)),
            dma((3, 2, 2)),
            dma((2,)),
        ],
        compiler_params=pltpu.CompilerParams(
            collective_id=2, has_side_effects=True, vmem_limit_bytes=58 * 2**20
        ),
    )(
        jnp.broadcast_to(gate_grad[None, :], (8, gate_grad.shape[0])),
        pick,
        kernels,
        columns,
        totals,
        logits,
        marks,
        features,
        tokens,
        router,
        rows,
        cotangent_rows,
        *deltas,
        slots,
        *weights,
    )


def per_device(ep, n_dp, tokens, cotangent, assign, w_router, w_gate, w_up, w_down):
    local_tokens = tokens[0]
    count, width = local_tokens.shape
    experts = w_router.shape[1]
    rows, cotangent_rows, rows_gate, pick, kernels, columns, totals, logits, marks, features = dispatch(
        local_tokens, cotangent[0], assign[0], w_router, ep
    )
    gate_matrix, up_matrix, down_matrix = w_gate[0], w_up[0], w_down[0]

    named = jnp.any(
        assign[0][:, :, None] == jnp.arange(experts, dtype=jnp.int32), axis=1
    ).astype(bf16)
    order = jnp.arange(count)
    earlier = (order[:, None] > order[None, :]).astype(bf16)
    rank = jnp.dot(earlier, named, preferred_element_type=f32)
    slot_of = jnp.where(named > 0, rank, -1.0)
    token_slots = (
        (slot_of[:, :, None] == jnp.arange(SLOTS, dtype=f32))
        .astype(bf16)
        .reshape(count, experts * SLOTS)
    )

    gate_linear = jnp.dot(rows, gate_matrix, preferred_element_type=f32)
    up_linear = jnp.dot(rows, up_matrix, preferred_element_type=f32)
    sigmoid_gate = jax.nn.sigmoid(gate_linear)
    activation = gate_linear * sigmoid_gate
    product = activation * up_linear
    hidden = product.astype(bf16)
    weighted = (rows_gate * product).astype(bf16)
    raw_back = jnp.dot(cotangent_rows, down_matrix, preferred_element_type=f32)
    gate_grad = jnp.sum(raw_back * hidden.astype(f32), axis=1).astype(bf16)
    scaled_back = rows_gate * raw_back
    up_delta = (scaled_back * activation).astype(bf16)
    gate_delta = (
        scaled_back * up_linear * sigmoid_gate * (1.0 + gate_linear * (1.0 - sigmoid_gate))
    ).astype(bf16)
    grad_tokens, grad_router, grad_gate, grad_up, grad_down = backward(
        gate_grad,
        pick,
        (kernels, columns, totals, logits, marks),
        features,
        local_tokens,
        w_router,
        rows,
        cotangent_rows,
        (gate_delta, up_delta, weighted),
        token_slots,
        (gate_matrix, up_matrix),
        ep,
        n_dp,
    )
    return grad_tokens[None], grad_router, grad_gate[None], grad_up[None], grad_down[None]


def solution(mesh):
    return jax.shard_map(
        functools.partial(per_device, mesh.shape["ep"], mesh.shape["dp"]),
        mesh=mesh,
        in_specs=(
            P("dp", "ep", None),
            P("dp", "ep", None),
            P("dp", "ep", None),
            P(),
            P("ep", None, None),
            P("ep", None, None),
            P("ep", None, None),
        ),
        out_specs=(
            P("dp", "ep", None),
            P(),
            P("ep", "dp", None),
            P("ep", "dp", None),
            P("ep", "dp", None),
        ),
        check_vma=False,
    )
```

```python
import functools
import heapq

import jax
import jax.numpy as jnp
from jax import lax
from jax.experimental import pallas as pl
from jax.experimental.pallas import tpu as pltpu
from jax.sharding import PartitionSpec as P

ITERS = 3
SLOTS = 8
LANES = 128
GROUP = 256
MESH = pl.DeviceIdType.MESH
f32 = jnp.float32
bf16 = jnp.bfloat16

cos_scale = 48.0
eps_norm = 1e-06
contract_first = (((0,), (0,)), ((), ()))
contract_last = (((1,), (1,)), ((), ()))


def torus_of(ep):
    ny = max(1, min(4, ep // 4))
    return ny, ep // (2 * ny)


def gather_plan(ny, nz, unit_us, hop_us=1.0):
    def half(part, side):
        return side if part is None else (part if part == side else -1)

    def spread(which, a, b, part):
        na, nb = (nz, ny) if which % 2 == 0 else (ny, nz)
        out = []

        def along(axis, n, at, signs):
            for sign in signs:
                last = abs(at) + 1 == n // 2
                piece = half(part, 0 if sign > 0 else 1) if last else part
                if piece != -1:
                    out.append((axis, sign, piece))

        def onward(at, n):
            if n == 1:
                return ()
            if at == 0:
                return (1, -1)
            return ((1,) if at > 0 else (-1,)) if abs(at) < n // 2 else ()

        if b == 0:
            along(0, na, a, onward(a, na))
        along(1, nb, b, onward(b, nb))
        return out

    heap, order, free, steps, ids = [], 0, {}, [], 0
    for which in range(len(unit_us)):
        heapq.heappush(heap, (0.0, order, None, which, 0, 0, None))
        order += 1
    while heap:
        now, _, arrival, which, a, b, part = heapq.heappop(heap)
        dy, dz = (b, a) if which % 2 == 0 else (a, b)
        sends = []
        for axis, sign, piece in spread(which, a, b, part):
            link = "zy"[axis] if which % 2 == 0 else "yz"[axis]
            share = 1.0 if piece is None else 0.5
            end = max(now, free.get((link, sign), 0.0)) + unit_us[which] * share
            free[(link, sign)] = end
            na, nb = (a + sign, b) if axis == 0 else (a, b + sign)
            heapq.heappush(heap, (end + hop_us, order, ids, which, na, nb, piece))
            sends.append((ids, which, dy, dz, part if piece is None else piece, link, sign))
            order += 1
            ids += 1
        sends.append((ids, which, dy, dz, part, "mate", 0))
        ids += 1
        steps.append((None if arrival is None else (arrival, which, dy, dz, part), sends))
    return steps, ids


def pieces_of(width):
    extra = max(LANES, width * 3 // 16 // LANES * LANES)
    return ((0, 0, width), (1, extra, width - extra), (1, 0, extra))


def unit_times(width):
    return tuple(2.8 * columns / width for _, _, columns in pieces_of(width))


def place(ep, ny, nz):
    me = lax.axis_index("ep")
    core = lax.rem(me, 2)
    chip = me // 2
    return me, core, chip // nz, lax.rem(chip, nz)


def at_ep(nz, y, z, core):
    return (y * nz + z) * 2 + core


def split_three(value):
    high = value.astype(bf16)
    rest = value - high.astype(f32)
    middle = rest.astype(bf16)
    return high, middle, (rest - middle.astype(f32)).astype(bf16)


def balance(meta, kernels, columns, totals, logits, marks, per_group):
    experts, total = logits.shape
    for g in range(total // GROUP):
        blocks = [meta[b % 2, b // 2] for b in range(g * per_group, (g + 1) * per_group)]
        flipped = jnp.concatenate(blocks, axis=0).T
        logits[:, g * GROUP : (g + 1) * GROUP] = flipped[:experts]
        marks[:, g * GROUP : (g + 1) * GROUP] = flipped[experts:]
    kernels[0] = jnp.exp(logits[...])
    for s in range(ITERS):
        kernel = kernels[s]
        column = jnp.sum(kernel, axis=1, keepdims=True)
        scaled = kernel / column
        row = jnp.sum(scaled, axis=0, keepdims=True)
        kernels[s + 1] = scaled / row
        columns[s] = jnp.broadcast_to(column, (experts, LANES))
        totals[s : s + 1, :] = row
    picked = jnp.where(marks[...] > 0.0, kernels[ITERS], 0.0)
    totals[ITERS : ITERS + 1, :] = jnp.sum(picked, axis=0, keepdims=True)
    totals[ITERS + 1 : ITERS + 2, :] = jnp.max(marks[...], axis=0, keepdims=True)


def moe_kernel(
    ep,
    n_dp,
    tok_ref,
    cot_ref,
    assign_ref,
    router_ref,
    w_gate_hbm,
    w_up_hbm,
    w_down_hbm,
    tokens_out,
    router_out,
    gate_out,
    up_out,
    down_out,
    tok_all,
    cot_all,
    meta,
    rows_tok,
    rows_cot,
    rows_gate,
    gate_grad,
    gate_delta,
    up_delta,
    weighted_rows,
    w_gate,
    w_up,
    w_down,
    row_mask,
    row_gate,
    pick,
    kernels,
    columns,
    totals,
    logits_all,
    marks,
    features_ref,
    slots_ref,
    table,
    grad,
    spread,
    turned,
    parts,
    shares,
    route_back,
    back_rows,
    got_far,
    got_near,
    meta_send,
    meta_recv,
    block_sends,
    block_recvs,
    sends,
    recvs,
    row_sends,
    row_recvs,
    far_sends,
    far_recvs,
    near_sends,
    near_recvs,
    weight_sems,
):
    ny, nz = torus_of(ep)
    count, width = tok_ref.shape
    experts = router_ref.shape[1]
    hidden_units = gate_delta.shape[1]
    total = ep * count
    groups = total // GROUP
    per_group = GROUP // count
    slots = per_group * SLOTS
    n_shares = width // LANES
    repeat = ep // n_shares
    chunk = width // n_dp // 2
    chunk_blocks = chunk // count
    ring = n_dp == 4
    dp = lax.axis_index("dp")
    me, core, y, z = place(ep, ny, nz)
    mine = y * nz + z
    mate = (dp, at_ep(nz, y, z, 1 - core))
    z_peers = [(dp, at_ep(nz, y, lax.rem(z + k, nz), core)) for k in range(1, nz)]
    y_peers = [(dp, at_ep(nz, lax.rem(y + k, ny), z, core)) for k in range(1, ny)]
    x_peers = [(lax.rem(dp + k, n_dp), me) for k in range(1, n_dp)]
    right, left = (lax.rem(dp + 1, n_dp), me), (lax.rem(dp + n_dp - 1, n_dp), me)
    share, twin = me // repeat, lax.rem(me, repeat)
    share_peers = [
        (dp, lax.rem(share + k, n_shares) * repeat + twin) for k in range(1, n_shares)
    ]

    barrier = pltpu.get_barrier_semaphore()

    def greet(k, carry):
        pl.semaphore_signal(
            barrier, inc=1, device_id=(dp, lax.rem(me + k, ep)), device_id_type=MESH
        )
        return carry

    lax.fori_loop(1, ep, greet, 0)
    for peer in x_peers:
        pl.semaphore_signal(barrier, inc=1, device_id=peer, device_id_type=MESH)
    fetches = [
        pltpu.make_async_copy(source, target, weight_sems.at[k])
        for k, (source, target) in enumerate(
            ((w_gate_hbm, w_gate), (w_up_hbm, w_up), (w_down_hbm, w_down))
        )
    ]
    for fetch in fetches:
        fetch.start()

    local = tok_ref[...]
    router = router_ref[...]
    tok_all[me] = local
    cot_all[me] = cot_ref[...]
    wide = local.astype(f32)
    inverse_local = 1.0 / jnp.sqrt(jnp.sum(wide * wide, axis=1, keepdims=True) + eps_norm)
    router_wide = router.astype(f32)
    square_row = jnp.sum(router_wide * router_wide, axis=0, keepdims=True) + eps_norm
    inner = jnp.dot(local, router, preferred_element_type=f32)
    logits = cos_scale * inner * inverse_local / jnp.sqrt(square_row)
    ids = lax.broadcasted_iota(jnp.int32, (count, experts), 1)
    routes = assign_ref[...]
    hit = jnp.zeros((count, experts), f32)
    for k in range(routes.shape[1]):
        hit = jnp.where(routes[:, k : k + 1] == ids, inverse_local, hit)
    meta[core, mine] = jnp.concatenate([logits, hit], axis=1)

    pl.semaphore_wait(barrier, ep - 1 + n_dp - 1)

    def meta_copy(n, block, blocks, peer, c=core):
        ref = meta.at[c, pl.ds(block, blocks)]
        return pltpu.make_async_remote_copy(
            src_ref=ref, dst_ref=ref, send_sem=meta_send.at[n], recv_sem=meta_recv.at[n],
            device_id=peer, device_id_type=MESH,
        )

    meta_copies = [meta_copy(k, mine, 1, p) for k, p in enumerate(z_peers)]
    for copy in meta_copies:
        copy.start()

    ends = {
        ("z", 1): (dp, at_ep(nz, y, lax.rem(z + 1, nz), core)),
        ("z", -1): (dp, at_ep(nz, y, lax.rem(z + nz - 1, nz), core)),
        ("y", 1): (dp, at_ep(nz, lax.rem(y + 1, ny), z, core)),
        ("y", -1): (dp, at_ep(nz, lax.rem(y + ny - 1, ny), z, core)),
        ("mate", 0): mate,
    }

    def view(which, dy, dz, part, c):
        block = at_ep(nz, lax.rem(y - dy + 2 * ny, ny), lax.rem(z - dz + 2 * nz, nz), c)
        first, rows = (0, count) if part is None else (part * (count // 2), count // 2)
        ref, column, columns_held = pieces_of(width)[which]
        held = (tok_all, cot_all)[ref]
        return held.at[block, pl.ds(first, rows), pl.ds(column, columns_held)]

    def block_copy(n, ref, end):
        return pltpu.make_async_remote_copy(
            src_ref=ref, dst_ref=ref, send_sem=block_sends.at[n], recv_sem=block_recvs.at[n],
            device_id=ends[end], device_id_type=MESH,
        )

    gather_copies, mate_arrivals = [], []

    def run(step):
        arrival, step_sends = step
        if arrival is not None:
            n, which, dy, dz, part = arrival
            block_copy(n, view(which, dy, dz, part, core), ("z", 1)).wait_recv()
        for n, which, dy, dz, part, link, sign in step_sends:
            copy = block_copy(n, view(which, dy, dz, part, core), (link, sign))
            copy.start()
            gather_copies.append(copy)
            if link == "mate":
                mate_arrivals.append((n, which, dy, dz, part))

    steps = gather_plan(ny, nz, unit_times(width))[0]
    first, second = len(steps) // 12, len(steps) // 6
    third, fourth = len(steps) // 4, len(steps) // 3
    for at, step in enumerate(steps):
        if at == first:
            for k in range(nz - 1):
                meta_copy(k, y * nz + lax.rem(z - 1 - k + nz, nz), 1, mate).wait_recv()
            for k, peer in enumerate(y_peers):
                meta_copies.append(meta_copy(nz - 1 + k, y * nz, nz, peer))
                meta_copies[-1].start()
        if at == second:
            for k in range(ny - 1):
                block = lax.rem(y - 1 - k + ny, ny) * nz
                meta_copy(nz - 1 + k, block, nz, mate).wait_recv()
            meta_copies.append(meta_copy(nz + ny - 2, 0, ny * nz, mate))
            meta_copies[-1].start()
        if at == third:
            meta_copy(nz + ny - 2, 0, ny * nz, mate, 1 - core).wait_recv()
            named = jnp.where(hit > 0.0, 1.0, 0.0)
            tokens_down = lax.broadcasted_iota(jnp.int32, (count, count), 0)
            tokens_across = lax.broadcasted_iota(jnp.int32, (count, count), 1)
            sooner = jnp.where(tokens_across < tokens_down, 1.0, 0.0).astype(bf16)
            rank = jnp.dot(sooner, named.astype(bf16), preferred_element_type=f32)
            slot_of = jnp.where(named > 0.0, rank, -1.0).astype(bf16)
            expert_down = lax.broadcasted_iota(jnp.int32, (experts, experts * SLOTS), 0)
            slot_across = lax.broadcasted_iota(jnp.int32, (experts, experts * SLOTS), 1)
            widen = jnp.where(slot_across // SLOTS == expert_down, 1.0, 0.0).astype(bf16)
            slot_wide = jnp.dot(slot_of, widen, preferred_element_type=f32)
            across = lax.broadcasted_iota(jnp.int32, (count, experts * SLOTS), 1)
            slots_ref[...] = jnp.where(
                slot_wide == lax.rem(across, SLOTS).astype(f32), 1.0, 0.0
            ).astype(bf16)
        if at == fourth:
            balance(meta, kernels, columns, totals, logits_all, marks, per_group)
            held = marks[pl.ds(me, 1), :] > 0.0
            kernel = jnp.where(held, kernels[ITERS, pl.ds(me, 1), :], 0.0)
            row_mask[...] = jnp.where(held, 1.0, 0.0)
            row_gate[...] = (kernel / totals[ITERS : ITERS + 1, :]).astype(bf16).astype(f32)
            before = lax.broadcasted_iota(jnp.int32, (GROUP, GROUP), 0)
            after = lax.broadcasted_iota(jnp.int32, (GROUP, GROUP), 1)
            earlier = jnp.where(
                (before < after) & (before // count == after // count), 1.0, 0.0
            ).astype(bf16)
            slot_ids = lax.broadcasted_iota(jnp.int32, (slots, GROUP), 0).astype(f32)
            base = (lax.broadcasted_iota(jnp.int32, (1, GROUP), 1) // count * SLOTS).astype(f32)
            for g in range(groups):
                mask = row_mask[:, g * GROUP : (g + 1) * GROUP]
                place_in = jnp.dot(
                    jnp.broadcast_to(mask, (8, GROUP)).astype(bf16), earlier,
                    preferred_element_type=f32,
                )[0:1]
                target = jnp.where(mask > 0.0, base + place_in, -1.0)
                chosen = jnp.where(slot_ids == target, 1.0, 0.0)
                rows_gate[g * slots : (g + 1) * slots, :] = jnp.sum(
                    chosen * row_gate[:, g * GROUP : (g + 1) * GROUP], axis=1, keepdims=True
                )
                pick[g] = chosen.astype(bf16)
        run(step)
    for n, which, dy, dz, part in mate_arrivals:
        block_copy(n, view(which, dy, dz, part, 1 - core), ("mate", 0)).wait_recv()

    def compact(g, carry):
        rows = pl.ds(pl.multiple_of(g * slots, slots), slots)
        blocks = pl.ds(g * per_group, per_group)
        rows_tok[rows, :] = jnp.dot(
            pick[g], tok_all[blocks].reshape(GROUP, width), preferred_element_type=f32
        ).astype(bf16)
        rows_cot[rows, :] = jnp.dot(
            pick[g], cot_all[blocks].reshape(GROUP, width), preferred_element_type=f32
        ).astype(bf16)
        return carry

    lax.fori_loop(0, groups, compact, 0)
    for fetch in fetches:
        fetch.wait()

    gate_grad[...] = jnp.zeros_like(gate_grad)
    row_step = min(256, ep * SLOTS)
    unit_step = min(256, hidden_units)
    row_steps = ep * SLOTS // row_step

    def expert(i, carry):
        rows = pl.ds(pl.multiple_of(lax.rem(i, row_steps) * row_step, row_step), row_step)
        units = pl.ds(pl.multiple_of(i // row_steps * unit_step, unit_step), unit_step)
        gate_linear = jnp.dot(rows_tok[rows, :], w_gate[:, units], preferred_element_type=f32)
        up_linear = jnp.dot(rows_tok[rows, :], w_up[:, units], preferred_element_type=f32)
        raw_back = jnp.dot(rows_cot[rows, :], w_down[:, units], preferred_element_type=f32)
        sigmoid_gate = jax.nn.sigmoid(gate_linear)
        activation = gate_linear * sigmoid_gate
        product = activation * up_linear
        gate = rows_gate[rows, :]
        weighted_rows[rows, units] = (gate * product).astype(bf16)
        gate_grad[rows, :] += jnp.sum(
            raw_back * product.astype(bf16).astype(f32), axis=1, keepdims=True
        )
        scaled_back = gate * raw_back
        up_delta[rows, units] = (scaled_back * activation).astype(bf16)
        gate_delta[rows, units] = (
            scaled_back * up_linear * sigmoid_gate * (1.0 + gate_linear * (1.0 - sigmoid_gate))
        ).astype(bf16)
        return carry

    lax.fori_loop(0, row_steps * (hidden_units // unit_step), expert, 0)
    features_ref[...] = tok_all[:, :, pl.ds(pl.multiple_of(share * LANES, LANES), LANES)]
    for copy in [*meta_copies, *gather_copies]:
        copy.wait_send()

    started = []
    across_table = width // hidden_units

    def buffer(n):
        held = (tok_all, cot_all)[n % 2]
        block, column = n // 2 // across_table, n // 2 % across_table
        return held.at[
            pl.ds(block * chunk_blocks, chunk_blocks),
            :,
            pl.ds(column * hidden_units, hidden_units),
        ]

    def far_buffer(a, side):
        return buffer(a * 2 + side)

    def near_buffer(a, side, half):
        return buffer(6 + a * 4 + side * 2 + half)

    def copy_of(n, ref, peer):
        return pltpu.make_async_remote_copy(
            src_ref=ref, dst_ref=ref, send_sem=sends.at[n], recv_sem=recvs.at[n],
            device_id=peer, device_id_type=MESH,
        )

    def start(copy):
        copy.start()
        started.append(copy)

    def far_copy(a, side):
        return pltpu.make_async_remote_copy(
            src_ref=far_buffer(a, side), dst_ref=got_far.at[a, side],
            send_sem=far_sends.at[a, side], recv_sem=far_recvs.at[a, side],
            device_id=(right, left)[side], device_id_type=MESH,
        )

    def near_copy(a, side, half):
        return pltpu.make_async_remote_copy(
            src_ref=near_buffer(a, side, half), dst_ref=got_near.at[a, side, half],
            send_sem=near_sends.at[a, side, half], recv_sem=near_recvs.at[a, side, half],
            device_id=(right, left)[side], device_id_type=MESH,
        )

    pairs = ((rows_cot, weighted_rows), (rows_tok, up_delta), (rows_tok, gate_delta))
    outs = (down_out, up_out, gate_out)
    arrays = range(3)

    def gradient(a, away, half):
        block = lax.rem(dp + away, n_dp)
        start_row = pl.multiple_of(block * (2 * chunk) + half * chunk, chunk)
        left_rows, right_rows = pairs[a]
        return lax.dot_general(
            left_rows[:, pl.ds(start_row, chunk)], right_rows[...], contract_first,
            preferred_element_type=f32,
        )

    def put(ref, value):
        ref[...] = value.astype(bf16).reshape(chunk_blocks, count, hidden_units)

    def far(a):
        for side in range(2):
            put(far_buffer(a, side), gradient(a, 2, side))
            start(far_copy(a, side))

    def near_plain(a):
        for side in range(2):
            put(near_buffer(a, side, 1 - side), gradient(a, (1, n_dp - 1)[side], 1 - side))
            start(near_copy(a, side, 1 - side))

    def near_joined(a):
        for side in range(2):
            mixed = gradient(a, (1, n_dp - 1)[side], side)
            far_copy(a, side).wait_recv()
            put(
                near_buffer(a, side, side),
                mixed + got_far[a, side].reshape(chunk, hidden_units).astype(f32),
            )
            start(near_copy(a, side, side))

    if ring:
        far(0)

    for g in range(groups):
        held = gate_grad[g * slots : (g + 1) * slots, :].astype(bf16).astype(f32)
        table[mine, core, g : g + 1, :] = jnp.sum(
            held * pick[g].astype(f32), axis=0, keepdims=True
        )
    n = 0

    def part(chip, chips):
        return table.at[pl.ds(chip, chips)]

    start(copy_of(n, table.at[mine, core], mate))
    if ring:
        far(1)
    copy_of(n, table.at[mine, 1 - core], mate).wait_recv()
    n += 1
    for k, peer in enumerate(z_peers):
        start(copy_of(n + k, part(mine, 1), peer))
    if ring:
        far(2)
    for k in range(nz - 1):
        copy_of(n + k, part(y * nz + lax.rem(z - 1 - k + nz, nz), 1), mate).wait_recv()
    n += nz - 1
    for k, peer in enumerate(y_peers):
        start(copy_of(n + k, part(y * nz, nz), peer))

    pieces = 4
    rows_each = ep // pieces

    def rows_back(q, carry):
        rows = pl.ds(pl.multiple_of(q * rows_each * SLOTS, rows_each * SLOTS), rows_each * SLOTS)
        value = lax.dot_general(
            gate_delta[rows, :], w_gate[...], contract_last, preferred_element_type=f32
        ) + lax.dot_general(up_delta[rows, :], w_up[...], contract_last, preferred_element_type=f32)
        route_back[pl.ds(q * rows_each, rows_each)] = value.astype(bf16).reshape(
            rows_each, SLOTS, width
        )
        return carry

    lax.fori_loop(0, pieces, rows_back, 0)

    def row_copy(k, from_block, to_block, peer):
        return pltpu.make_async_remote_copy(
            src_ref=route_back.at[from_block], dst_ref=back_rows.at[to_block],
            send_sem=row_sends.at[k], recv_sem=row_recvs.at[k],
            device_id=(dp, peer), device_id_type=MESH,
        )

    def send_rows(k, carry):
        peer = lax.rem(me + k, ep)
        row_copy(k, peer, me, peer).start()
        return carry

    lax.fori_loop(1, ep, send_rows, 0)
    back_rows[me] = route_back[me]

    for k in range(ny - 1):
        copy_of(n + k, part(lax.rem(y - 1 - k + ny, ny) * nz, nz), mate).wait_recv()
    n += ny - 1

    for g in range(groups):
        both = table[:, :, g, :]
        grad[:, g * GROUP : (g + 1) * GROUP] = both.reshape(experts, GROUP)
    inverse_token = totals[ITERS + 1 : ITERS + 2, :]
    picked_sum = totals[ITERS : ITERS + 1, :]
    member = marks[...] > 0.0
    route = jnp.where(member, grad[...], 0.0)
    gates = jnp.where(member, kernels[ITERS], 0.0) / picked_sum
    grad[...] = jnp.where(
        member, (route - jnp.sum(route * gates, axis=0, keepdims=True)) / picked_sum, 0.0
    )
    for s in reversed(range(ITERS)):
        kernel = kernels[s + 1]
        row = totals[s : s + 1, :]
        column = columns[s][:, 0:1]
        slope = grad[...]
        slope = (slope - jnp.sum(slope * kernel, axis=0, keepdims=True)) / row
        moment = jnp.sum(slope * (kernel * row), axis=1, keepdims=True)
        grad[...] = (slope - moment) / column
    logit_grad = grad[...] * kernels[0]
    weighted = logit_grad * logits_all[...]
    square = jnp.broadcast_to(square_row, (LANES, experts)).T[:, 0:1]
    turn = logit_grad * (cos_scale * inverse_token) / jnp.sqrt(square)
    spread[:experts, :] = turn
    spread[experts:, :] = jnp.broadcast_to(
        jnp.sum(weighted, axis=0, keepdims=True) * inverse_token * inverse_token,
        (spread.shape[0] - experts, total),
    )

    features = features_ref[...].reshape(total, LANES)
    product = jnp.dot(
        jnp.concatenate(split_three(turn), axis=0), features, preferred_element_type=f32
    )
    product = product[:experts] + product[experts : 2 * experts] + product[2 * experts :]
    own_router = router_ref[pl.ds(pl.multiple_of(share * LANES, LANES), LANES), :].astype(f32).T
    parts[dp] = product - own_router * (jnp.sum(weighted, axis=1, keepdims=True) / square)
    for k, peer in enumerate(x_peers):
        start(copy_of(n + k, parts.at[dp], peer))

    if ring:
        for a in arrays:
            near_plain(a)
        for a in arrays:
            near_joined(a)

    turned[...] = spread[:, pl.ds(pl.multiple_of(me * count // LANES * LANES, LANES), LANES)].T
    own = turned[pl.ds(pl.multiple_of(lax.rem(me, LANES // count) * count, count), count), :]
    back = jnp.zeros((count, width), f32)
    for term in split_three(own[:, :experts]):
        back += lax.dot_general(term, router, contract_last, preferred_element_type=f32)
    back -= tok_ref[...].astype(f32) * own[:, experts : experts + 1]

    for k in range(n_dp - 1):
        copy_of(n + k, parts.at[lax.rem(dp - 1 - k + n_dp, n_dp)], mate).wait_recv()
    n += n_dp - 1
    summed = parts[0]
    for k in range(1, n_dp):
        summed += parts[k]
    shares[share] = summed
    for k, peer in enumerate(share_peers):
        start(copy_of(n + k, shares.at[share], peer))

    def got_rows(k, carry):
        block = lax.rem(me - k + ep, ep)
        row_copy(k, block, block, block).wait_recv()
        return carry

    lax.fori_loop(1, ep, got_rows, 0)
    tokens_out[...] = (
        back
        + jnp.dot(
            slots_ref[...], back_rows[...].reshape(ep * SLOTS, width), preferred_element_type=f32
        )
    ).astype(bf16)

    for k in range(n_shares - 1):
        copy_of(n + k, shares.at[lax.rem(share - 1 - k + n_shares, n_shares)], mate).wait_recv()
    router_out[...] = shares[...]

    def finish(a, half):
        value = gradient(a, 0, half)
        if ring:
            for side in range(2):
                near_copy(a, side, half).wait_recv()
                value += got_near[a, side, half].reshape(chunk, hidden_units).astype(f32)
        outs[a][half * chunk : (half + 1) * chunk, :] = value.astype(bf16)

    for a in arrays:
        for half in range(2):
            finish(a, half)

    def sent_rows(k, carry):
        peer = lax.rem(me + k, ep)
        row_copy(k, peer, me, peer).wait_send()
        return carry

    lax.fori_loop(1, ep, sent_rows, 0)
    for copy in started:
        copy.wait_send()


def per_device(ep, n_dp, tokens, cotangent, assign, w_router, w_gate, w_up, w_down):
    ny, nz = torus_of(ep)
    _, count, width = tokens.shape
    experts = w_router.shape[1]
    hidden_units = w_gate.shape[2]
    total = ep * count
    groups = total // GROUP
    n_shares = width // LANES
    rows = ep * SLOTS
    chunk = width // n_dp // 2
    copies = 1 + nz - 1 + ny - 1 + n_dp - 1 + n_shares - 1
    blocks = gather_plan(ny, nz, unit_times(width))[1]
    shape, vmem_array, dma = jax.ShapeDtypeStruct, pltpu.VMEM, pltpu.SemaphoreType.DMA
    vmem = pl.BlockSpec(memory_space=pltpu.VMEM)
    anywhere = pl.BlockSpec(memory_space=pl.ANY)
    gradient = shape((2 * chunk, hidden_units), bf16)
    small = nz + ny - 1
    grad_tokens, shares, grad_gate, grad_up, grad_down = pl.pallas_call(
        functools.partial(moe_kernel, ep, n_dp),
        out_shape=(
            shape((count, width), bf16),
            shape((n_shares, experts, LANES), f32),
            gradient,
            gradient,
            gradient,
        ),
        in_specs=[vmem] * 4 + [anywhere] * 3,
        out_specs=(vmem,) * 5,
        scratch_shapes=[
            vmem_array((ep, count, width), bf16),
            vmem_array((ep, count, width), bf16),
            vmem_array((2, ny * nz, count, 2 * experts), f32),
            vmem_array((rows, width), bf16),
            vmem_array((rows, width), bf16),
            vmem_array((rows, 1), f32),
            vmem_array((rows, 1), f32),
            vmem_array((rows, hidden_units), bf16),
            vmem_array((rows, hidden_units), bf16),
            vmem_array((rows, hidden_units), bf16),
            vmem_array((width, hidden_units), bf16),
            vmem_array((width, hidden_units), bf16),
            vmem_array((width, hidden_units), bf16),
            vmem_array((1, total), f32),
            vmem_array((1, total), f32),
            vmem_array((groups, GROUP // count * SLOTS, GROUP), bf16),
            vmem_array((ITERS + 1, experts, total), f32),
            vmem_array((ITERS, experts, LANES), f32),
            vmem_array((8, total), f32),
            vmem_array((experts, total), f32),
            vmem_array((experts, total), f32),
            vmem_array((ep, count, LANES), bf16),
            vmem_array((count, experts * SLOTS), bf16),
            vmem_array((ny * nz, 2, groups, GROUP), f32),
            vmem_array((experts, total), f32),
            vmem_array((LANES, total), f32),
            vmem_array((LANES, LANES), f32),
            vmem_array((n_dp, experts, LANES), f32),
            vmem_array((n_shares, experts, LANES), f32),
            vmem_array((ep, SLOTS, width), bf16),
            vmem_array((ep, SLOTS, width), bf16),
            vmem_array((3, 2, chunk // count, count, hidden_units), bf16),
            vmem_array((3, 2, 2, chunk // count, count, hidden_units), bf16),
            dma((small,)),
            dma((small,)),
            dma((blocks,)),
            dma((blocks,)),
            dma((copies,)),
            dma((copies,)),
            dma((ep,)),
            dma((ep,)),
            dma((3, 2)),
            dma((3, 2)),
            dma((3, 2, 2)),
            dma((3, 2, 2)),
            dma((3,)),
        ],
        compiler_params=pltpu.CompilerParams(
            collective_id=1, has_side_effects=True, vmem_limit_bytes=60 * 2**20
        ),
    )(tokens[0], cotangent[0], assign[0], w_router, w_gate[0], w_up[0], w_down[0])
    grad_router = shares.transpose(0, 2, 1).reshape(width, experts)
    return grad_tokens[None], grad_router, grad_gate[None], grad_up[None], grad_down[None]


def solution(mesh):
    return jax.shard_map(
        functools.partial(per_device, mesh.shape["ep"], mesh.shape["dp"]),
        mesh=mesh,
        in_specs=(
            P("dp", "ep", None),
            P("dp", "ep", None),
            P("dp", "ep", None),
            P(),
            P("ep", None, None),
            P("ep", None, None),
            P("ep", None, None),
        ),
        out_specs=(
            P("dp", "ep", None),
            P(),
            P("ep", "dp", None),
            P("ep", "dp", None),
            P("ep", "dp", None),
        ),
        check_vma=False,
    )
```

```python
import functools
import heapq

import jax
import jax.numpy as jnp
from jax import lax
from jax.experimental import pallas as pl
from jax.experimental.pallas import tpu as pltpu
from jax.sharding import PartitionSpec as P

ITERS = 3
SLOTS = 8
LANES = 128
GROUP = 256
MESH = pl.DeviceIdType.MESH
f32 = jnp.float32
bf16 = jnp.bfloat16

cos_scale = 48.0
eps_norm = 1e-06
contract_first = (((0,), (0,)), ((), ()))
contract_last = (((1,), (1,)), ((), ()))


def torus_of(ep):
    ny = max(1, min(4, ep // 4))
    return ny, ep // (2 * ny)


def gather_plan(ny, nz, unit_us, begin_us, hop_us=1.0):
    def half(part, side):
        return side if part is None else (part if part == side else -1)

    def spread(which, a, b, part):
        na, nb = (nz, ny) if which % 2 == 0 else (ny, nz)
        out = []

        def along(axis, n, at, signs):
            for sign in signs:
                last = abs(at) + 1 == n // 2
                piece = half(part, 0 if sign > 0 else 1) if last else part
                if piece != -1:
                    out.append((axis, sign, piece))

        def onward(at, n):
            if n == 1:
                return ()
            if at == 0:
                return (1, -1)
            return ((1,) if at > 0 else (-1,)) if abs(at) < n // 2 else ()

        if b == 0:
            along(0, na, a, onward(a, na))
        along(1, nb, b, onward(b, nb))
        return out

    heap, order, free, steps, ids = [], 0, {}, [], 0
    for which in range(len(unit_us)):
        heapq.heappush(heap, (begin_us[which], order, None, which, 0, 0, None))
        order += 1
    while heap:
        now, _, arrival, which, a, b, part = heapq.heappop(heap)
        dy, dz = (b, a) if which % 2 == 0 else (a, b)
        sends = []
        for axis, sign, piece in spread(which, a, b, part):
            link = "zy"[axis] if which % 2 == 0 else "yz"[axis]
            share = 1.0 if piece is None else 0.5
            end = max(now, free.get((link, sign), 0.0)) + unit_us[which] * share
            free[(link, sign)] = end
            na, nb = (a + sign, b) if axis == 0 else (a, b + sign)
            heapq.heappush(heap, (end + hop_us, order, ids, which, na, nb, piece))
            sends.append((ids, which, dy, dz, part if piece is None else piece, link, sign))
            order += 1
            ids += 1
        sends.append((ids, which, dy, dz, part, "mate", 0))
        ids += 1
        steps.append((None if arrival is None else (arrival, which, dy, dz, part), sends))
    return steps, ids


def pieces_of(width):
    split = width * 5 // 8 // LANES * LANES
    return tuple(
        (held, column, columns)
        for held in (0, 1)
        for column, columns in ((0, split), (split, width - split))
    )


def plan_of(ny, nz, width):
    times = tuple(2.8 * columns / width for _, _, columns in pieces_of(width))
    return gather_plan(ny, nz, times, (0.0, 0.0, 4.0, 4.0))


def place(ep, ny, nz):
    me = lax.axis_index("ep")
    core = lax.rem(me, 2)
    chip = me // 2
    return me, core, chip // nz, lax.rem(chip, nz)


def at_ep(nz, y, z, core):
    return (y * nz + z) * 2 + core


def split_three(value):
    high = value.astype(bf16)
    rest = value - high.astype(f32)
    middle = rest.astype(bf16)
    return high, middle, (rest - middle.astype(f32)).astype(bf16)


def balance(meta, kernels, columns, totals, marks, per_group):
    experts, total = marks.shape
    for g in range(total // GROUP):
        blocks = []
        for b in range(g * per_group, (g + 1) * per_group):
            block = meta[b % 2, b // 2]
            blocks += [block[:, :experts], block[:, experts:]]
        flipped = jnp.concatenate(blocks, axis=0).T
        marks[:, g * GROUP : (g + 1) * GROUP] = flipped
    kernels[0] = jnp.abs(marks[...])
    for s in range(ITERS):
        kernel = kernels[s]
        column = jnp.sum(kernel, axis=1, keepdims=True)
        scaled = kernel / column
        row = jnp.sum(scaled, axis=0, keepdims=True)
        kernels[s + 1] = scaled / row
        columns[s] = jnp.broadcast_to(column, (experts, LANES))
        totals[s : s + 1, :] = row
    picked = jnp.where(marks[...] < 0.0, kernels[ITERS], 0.0)
    totals[ITERS : ITERS + 1, :] = jnp.sum(picked, axis=0, keepdims=True)


def moe_kernel(
    ep,
    n_dp,
    tok_ref,
    cot_ref,
    assign_ref,
    router_ref,
    w_gate_hbm,
    w_up_hbm,
    w_down_hbm,
    tokens_out,
    router_out,
    gate_out,
    up_out,
    down_out,
    tok_all,
    cot_all,
    meta,
    rows_tok,
    rows_cot,
    rows_gate,
    gate_grad,
    gate_delta,
    up_delta,
    weighted_rows,
    w_gate,
    w_up,
    w_down,
    row_mask,
    row_gate,
    pick,
    kernels,
    columns,
    totals,
    marks,
    slots_ref,
    gate_all,
    up_all,
    spare,
    table,
    grad,
    spread,
    turned,
    parts,
    shares,
    route_back,
    back_rows,
    got_far,
    got_near,
    meta_send,
    meta_recv,
    block_sends,
    block_recvs,
    sends,
    recvs,
    row_sends,
    row_recvs,
    far_sends,
    far_recvs,
    near_sends,
    near_recvs,
    weight_sems,
):
    ny, nz = torus_of(ep)
    count, width = tok_ref.shape
    experts = router_ref.shape[0]
    hidden_units = gate_delta.shape[1]
    total = ep * count
    groups = total // GROUP
    per_group = GROUP // count
    slots = per_group * SLOTS
    n_shares = width // LANES
    repeat = ep // n_shares
    chunk = width // n_dp // 2
    chunk_blocks = chunk // count
    ring = n_dp == 4
    dp = lax.axis_index("dp")
    me, core, y, z = place(ep, ny, nz)
    mine = y * nz + z
    mate = (dp, at_ep(nz, y, z, 1 - core))
    z_peers = [(dp, at_ep(nz, y, lax.rem(z + k, nz), core)) for k in range(1, nz)]
    y_peers = [(dp, at_ep(nz, lax.rem(y + k, ny), z, core)) for k in range(1, ny)]
    x_peers = [(lax.rem(dp + k, n_dp), me) for k in range(1, n_dp)]
    right, left = (lax.rem(dp + 1, n_dp), me), (lax.rem(dp + n_dp - 1, n_dp), me)
    share, twin = me // repeat, lax.rem(me, repeat)
    share_peers = [
        (dp, lax.rem(share + k, n_shares) * repeat + twin) for k in range(1, n_shares)
    ]

    barrier = pltpu.get_barrier_semaphore()

    def greet(k, carry):
        pl.semaphore_signal(
            barrier, inc=1, device_id=(dp, lax.rem(me + k, ep)), device_id_type=MESH
        )
        return carry

    lax.fori_loop(1, ep, greet, 0)
    for peer in x_peers:
        pl.semaphore_signal(barrier, inc=1, device_id=peer, device_id_type=MESH)
    fetches = [
        pltpu.make_async_copy(source, target, weight_sems.at[k])
        for k, (source, target) in enumerate(
            ((w_gate_hbm, w_gate), (w_up_hbm, w_up), (w_down_hbm, w_down))
        )
    ]
    for fetch in fetches:
        fetch.start()

    local = tok_ref[...]
    router = router_ref[...]
    tok_all[me] = local
    cot_all[me] = cot_ref[...]
    wide = local.astype(f32)
    inverse_local = 1.0 / jnp.sqrt(jnp.sum(wide * wide, axis=1, keepdims=True) + eps_norm)
    router_wide = router.astype(f32)
    square = jnp.sum(router_wide * router_wide, axis=1, keepdims=True) + eps_norm
    square_row = jnp.broadcast_to(square, (experts, LANES)).T[0:1, :]
    inner = lax.dot_general(local, router, contract_last, preferred_element_type=f32)
    logits = cos_scale * inner * inverse_local / jnp.sqrt(square_row)
    ids = lax.broadcasted_iota(jnp.int32, (count, experts), 1).astype(f32)
    routes = assign_ref[...].astype(f32).T
    named = jnp.zeros((count, experts), f32)
    for k in range(routes.shape[1]):
        named = jnp.where(routes[:, k : k + 1] == ids, 1.0, named)
    start_kernel = jnp.exp(logits)
    signed = jnp.where(named > 0.0, -start_kernel, start_kernel)
    meta[core, mine] = jnp.concatenate([signed[: count // 2], signed[count // 2 :]], axis=1)

    pl.semaphore_wait(barrier, ep - 1 + n_dp - 1)

    def meta_copy(n, block, blocks, peer, c=core):
        ref = meta.at[c, pl.ds(block, blocks)]
        return pltpu.make_async_remote_copy(
            src_ref=ref, dst_ref=ref, send_sem=meta_send.at[n], recv_sem=meta_recv.at[n],
            device_id=peer, device_id_type=MESH,
        )

    meta_copies = [meta_copy(k, mine, 1, p) for k, p in enumerate(z_peers)]
    for copy in meta_copies:
        copy.start()

    ends = {
        ("z", 1): (dp, at_ep(nz, y, lax.rem(z + 1, nz), core)),
        ("z", -1): (dp, at_ep(nz, y, lax.rem(z + nz - 1, nz), core)),
        ("y", 1): (dp, at_ep(nz, lax.rem(y + 1, ny), z, core)),
        ("y", -1): (dp, at_ep(nz, lax.rem(y + ny - 1, ny), z, core)),
        ("mate", 0): mate,
    }

    def view(which, dy, dz, part, c):
        block = at_ep(nz, lax.rem(y - dy + 2 * ny, ny), lax.rem(z - dz + 2 * nz, nz), c)
        first, rows = (0, count) if part is None else (part * (count // 2), count // 2)
        ref, column, columns_held = pieces_of(width)[which]
        held = (tok_all, cot_all)[ref]
        return held.at[block, pl.ds(first, rows), pl.ds(column, columns_held)]

    def block_copy(n, ref, end):
        return pltpu.make_async_remote_copy(
            src_ref=ref, dst_ref=ref, send_sem=block_sends.at[n], recv_sem=block_recvs.at[n],
            device_id=ends[end], device_id_type=MESH,
        )

    gather_copies, mate_arrivals = [], []

    def run(step):
        arrival, step_sends = step
        if arrival is not None:
            n, which, dy, dz, part = arrival
            block_copy(n, view(which, dy, dz, part, core), ("z", 1)).wait_recv()
        for n, which, dy, dz, part, link, sign in step_sends:
            copy = block_copy(n, view(which, dy, dz, part, core), (link, sign))
            copy.start()
            gather_copies.append(copy)
            if link == "mate":
                mate_arrivals.append((n, which, dy, dz, part))

    steps = plan_of(ny, nz, width)[0]

    def compact(held, rows_ref, g):
        blocks = held[g * per_group : (g + 1) * per_group].reshape(GROUP, width)
        rows_ref[g * slots : (g + 1) * slots, :] = jnp.dot(
            pick[g], blocks, preferred_element_type=f32
        ).astype(bf16)

    row_step = min(256, ep * SLOTS)
    unit_step = min(256, hidden_units)
    row_steps = ep * SLOTS // row_step
    expert_steps = row_steps * (hidden_units // unit_step)

    def tile(i):
        row, unit = i % row_steps * row_step, i // row_steps * unit_step
        return slice(row, row + row_step), slice(unit, unit + unit_step)

    def forward(i):
        rows, units = tile(i)
        gate_linear = jnp.dot(rows_tok[rows, :], w_gate[:, units], preferred_element_type=f32)
        up_linear = jnp.dot(rows_tok[rows, :], w_up[:, units], preferred_element_type=f32)
        gate_all[rows, units] = gate_linear
        up_all[rows, units] = up_linear
        product = gate_linear * jax.nn.sigmoid(gate_linear) * up_linear
        weighted_rows[rows, units] = (rows_gate[rows, :] * product).astype(bf16)

    def norms(g):
        values = tok_all[g * per_group : (g + 1) * per_group].reshape(GROUP, width).astype(f32)
        inverse = 1.0 / jnp.sqrt(jnp.sum(values * values, axis=1, keepdims=True) + eps_norm)
        totals[ITERS + 1 : ITERS + 2, g * GROUP : (g + 1) * GROUP] = jnp.broadcast_to(
            inverse, (GROUP, LANES)
        ).T[0:1, :]

    def mates(wanted):
        for n, which, dy, dz, part in mate_arrivals:
            if pieces_of(width)[which][0] == wanted:
                block_copy(n, view(which, dy, dz, part, 1 - core), ("mate", 0)).wait_recv()

    def fetched():
        for fetch in fetches:
            fetch.wait()

    token_work = [functools.partial(compact, tok_all, rows_tok, g) for g in range(groups)]
    token_work += [fetched]
    token_work += [functools.partial(forward, i) for i in range(expert_steps)]
    token_work += [functools.partial(norms, g) for g in range(groups)]
    tokens_in = max(
        at for at, step in enumerate(steps) if pieces_of(width)[step[0][1] if step[0] else 0][0] == 0
    )
    first, second = tokens_in // 6, tokens_in // 3
    third, fourth = tokens_in // 2, tokens_in * 2 // 3
    ready = min(tokens_in + 4, len(steps) - 1)
    for at, step in enumerate(steps):
        if at == first:
            for k in range(nz - 1):
                meta_copy(k, y * nz + lax.rem(z - 1 - k + nz, nz), 1, mate).wait_recv()
            for k, peer in enumerate(y_peers):
                meta_copies.append(meta_copy(nz - 1 + k, y * nz, nz, peer))
                meta_copies[-1].start()
        if at == second:
            for k in range(ny - 1):
                block = lax.rem(y - 1 - k + ny, ny) * nz
                meta_copy(nz - 1 + k, block, nz, mate).wait_recv()
            meta_copies.append(meta_copy(nz + ny - 2, 0, ny * nz, mate))
            meta_copies[-1].start()
        if at == third:
            meta_copy(nz + ny - 2, 0, ny * nz, mate, 1 - core).wait_recv()
            tokens_down = lax.broadcasted_iota(jnp.int32, (count, count), 0)
            tokens_across = lax.broadcasted_iota(jnp.int32, (count, count), 1)
            sooner = jnp.where(tokens_across < tokens_down, 1.0, 0.0).astype(bf16)
            rank = jnp.dot(sooner, named.astype(bf16), preferred_element_type=f32)
            slot_of = jnp.where(named > 0.0, rank, -1.0).astype(bf16)
            expert_down = lax.broadcasted_iota(jnp.int32, (experts, experts * SLOTS), 0)
            slot_across = lax.broadcasted_iota(jnp.int32, (experts, experts * SLOTS), 1)
            widen = jnp.where(slot_across // SLOTS == expert_down, 1.0, 0.0).astype(bf16)
            slot_wide = jnp.dot(slot_of, widen, preferred_element_type=f32)
            across = lax.broadcasted_iota(jnp.int32, (count, experts * SLOTS), 1)
            slots_ref[...] = jnp.where(
                slot_wide == lax.rem(across, SLOTS).astype(f32), 1.0, 0.0
            ).astype(bf16)
        if at == fourth:
            balance(meta, kernels, columns, totals, marks, per_group)
            held = marks[pl.ds(me, 1), :] < 0.0
            kernel = jnp.where(held, kernels[ITERS, pl.ds(me, 1), :], 0.0)
            row_mask[...] = jnp.where(held, 1.0, 0.0)
            row_gate[...] = (kernel / totals[ITERS : ITERS + 1, :]).astype(bf16).astype(f32)
            before = lax.broadcasted_iota(jnp.int32, (GROUP, GROUP), 0)
            after = lax.broadcasted_iota(jnp.int32, (GROUP, GROUP), 1)
            earlier = jnp.where(
                (before < after) & (before // count == after // count), 1.0, 0.0
            ).astype(bf16)
            slot_ids = lax.broadcasted_iota(jnp.int32, (slots, GROUP), 0).astype(f32)
            base = (lax.broadcasted_iota(jnp.int32, (1, GROUP), 1) // count * SLOTS).astype(f32)
            for g in range(groups):
                mask = row_mask[:, g * GROUP : (g + 1) * GROUP]
                place_in = jnp.dot(
                    jnp.broadcast_to(mask, (8, GROUP)).astype(bf16), earlier,
                    preferred_element_type=f32,
                )[0:1]
                target = jnp.where(mask > 0.0, base + place_in, -1.0)
                chosen = jnp.where(slot_ids == target, 1.0, 0.0)
                rows_gate[g * slots : (g + 1) * slots, :] = jnp.sum(
                    chosen * row_gate[:, g * GROUP : (g + 1) * GROUP], axis=1, keepdims=True
                )
                pick[g] = chosen.astype(bf16)
        if at == ready:
            mates(0)
        if at > ready:
            share_of = -(-len(token_work) // max(1, len(steps) - at))
            for work in token_work[:share_of]:
                work()
            token_work = token_work[share_of:]
        run(step)
    for work in token_work:
        work()
    mates(1)
    for g in range(groups):
        compact(cot_all, rows_cot, g)

    started = []
    across_table = width // hidden_units

    def buffer(n):
        if n < 2:
            return spare.at[n]
        block, column = (n - 2) // across_table, (n - 2) % across_table
        return cot_all.at[
            pl.ds(block * chunk_blocks, chunk_blocks),
            :,
            pl.ds(column * hidden_units, hidden_units),
        ]

    def far_buffer(a, side):
        return buffer(a * 2 + side)

    def near_buffer(a, side, half):
        return buffer(6 + a * 4 + side * 2 + half)

    def copy_of(n, ref, peer):
        return pltpu.make_async_remote_copy(
            src_ref=ref, dst_ref=ref, send_sem=sends.at[n], recv_sem=recvs.at[n],
            device_id=peer, device_id_type=MESH,
        )

    def start(copy):
        copy.start()
        started.append(copy)

    def far_copy(a, side):
        return pltpu.make_async_remote_copy(
            src_ref=far_buffer(a, side), dst_ref=got_far.at[a, side],
            send_sem=far_sends.at[a, side], recv_sem=far_recvs.at[a, side],
            device_id=(right, left)[side], device_id_type=MESH,
        )

    def near_copy(a, side, half):
        return pltpu.make_async_remote_copy(
            src_ref=near_buffer(a, side, half), dst_ref=got_near.at[a, side, half],
            send_sem=near_sends.at[a, side, half], recv_sem=near_recvs.at[a, side, half],
            device_id=(right, left)[side], device_id_type=MESH,
        )

    pairs = ((rows_cot, weighted_rows), (rows_tok, up_delta), (rows_tok, gate_delta))
    outs = (down_out, up_out, gate_out)
    arrays = range(3)

    def gradient(a, away, half):
        block = lax.rem(dp + away, n_dp)
        start_row = pl.multiple_of(block * (2 * chunk) + half * chunk, chunk)
        left_rows, right_rows = pairs[a]
        return lax.dot_general(
            left_rows[:, pl.ds(start_row, chunk)], right_rows[...], contract_first,
            preferred_element_type=f32,
        )

    def put(ref, value):
        ref[...] = value.astype(bf16).reshape(chunk_blocks, count, hidden_units)

    def far(a):
        for side in range(2):
            put(far_buffer(a, side), gradient(a, 2, side))
            start(far_copy(a, side))

    def near_plain(a):
        for side in range(2):
            put(near_buffer(a, side, 1 - side), gradient(a, (1, n_dp - 1)[side], 1 - side))
            start(near_copy(a, side, 1 - side))

    def near_joined(a):
        for side in range(2):
            mixed = gradient(a, (1, n_dp - 1)[side], side)
            far_copy(a, side).wait_recv()
            put(
                near_buffer(a, side, side),
                mixed + got_far[a, side].reshape(chunk, hidden_units).astype(f32),
            )
            start(near_copy(a, side, side))

    if ring:
        far(0)

    gate_grad[...] = jnp.zeros_like(gate_grad)

    def expert(i, carry):
        rows = pl.ds(pl.multiple_of(lax.rem(i, row_steps) * row_step, row_step), row_step)
        units = pl.ds(pl.multiple_of(i // row_steps * unit_step, unit_step), unit_step)
        raw_back = jnp.dot(rows_cot[rows, :], w_down[:, units], preferred_element_type=f32)
        gate_linear = gate_all[rows, units]
        up_linear = up_all[rows, units]
        sigmoid_gate = jax.nn.sigmoid(gate_linear)
        activation = gate_linear * sigmoid_gate
        product = activation * up_linear
        gate_grad[rows, :] += jnp.sum(
            raw_back * product.astype(bf16).astype(f32), axis=1, keepdims=True
        )
        scaled_back = rows_gate[rows, :] * raw_back
        up_delta[rows, units] = (scaled_back * activation).astype(bf16)
        gate_delta[rows, units] = (
            scaled_back * up_linear * sigmoid_gate * (1.0 + gate_linear * (1.0 - sigmoid_gate))
        ).astype(bf16)
        return carry

    lax.fori_loop(0, expert_steps, expert, 0)
    for copy in [*meta_copies, *gather_copies]:
        copy.wait_send()

    for g in range(groups):
        held = gate_grad[g * slots : (g + 1) * slots, :].astype(bf16).astype(f32)
        table[mine, core, g : g + 1, :] = jnp.sum(
            held * pick[g].astype(f32), axis=0, keepdims=True
        )
    n = 0

    def part(chip, chips):
        return table.at[pl.ds(chip, chips)]

    start(copy_of(n, table.at[mine, core], mate))
    if ring:
        far(1)
    copy_of(n, table.at[mine, 1 - core], mate).wait_recv()
    n += 1
    for k, peer in enumerate(z_peers):
        start(copy_of(n + k, part(mine, 1), peer))
    if ring:
        far(2)
    for k in range(nz - 1):
        copy_of(n + k, part(y * nz + lax.rem(z - 1 - k + nz, nz), 1), mate).wait_recv()
    n += nz - 1
    for k, peer in enumerate(y_peers):
        start(copy_of(n + k, part(y * nz, nz), peer))

    pieces = 4
    rows_each = ep // pieces

    def rows_back(q, carry):
        rows = pl.ds(pl.multiple_of(q * rows_each * SLOTS, rows_each * SLOTS), rows_each * SLOTS)
        value = lax.dot_general(
            gate_delta[rows, :], w_gate[...], contract_last, preferred_element_type=f32
        ) + lax.dot_general(up_delta[rows, :], w_up[...], contract_last, preferred_element_type=f32)
        route_back[pl.ds(q * rows_each, rows_each)] = value.astype(bf16).reshape(
            rows_each, SLOTS, width
        )
        return carry

    lax.fori_loop(0, pieces, rows_back, 0)

    def row_copy(k, from_block, to_block, peer):
        return pltpu.make_async_remote_copy(
            src_ref=route_back.at[from_block], dst_ref=back_rows.at[to_block],
            send_sem=row_sends.at[k], recv_sem=row_recvs.at[k],
            device_id=(dp, peer), device_id_type=MESH,
        )

    def send_rows(k, carry):
        peer = lax.rem(me + k, ep)
        row_copy(k, peer, me, peer).start()
        return carry

    lax.fori_loop(1, ep, send_rows, 0)
    back_rows[me] = route_back[me]

    for k in range(ny - 1):
        copy_of(n + k, part(lax.rem(y - 1 - k + ny, ny) * nz, nz), mate).wait_recv()
    n += ny - 1

    for g in range(groups):
        both = table[:, :, g, :]
        grad[:, g * GROUP : (g + 1) * GROUP] = both.reshape(experts, GROUP)
    inverse_token = totals[ITERS + 1 : ITERS + 2, :]
    picked_sum = totals[ITERS : ITERS + 1, :]
    member = marks[...] < 0.0
    route = jnp.where(member, grad[...], 0.0)
    gates = jnp.where(member, kernels[ITERS], 0.0) / picked_sum
    grad[...] = jnp.where(
        member, (route - jnp.sum(route * gates, axis=0, keepdims=True)) / picked_sum, 0.0
    )
    for s in reversed(range(ITERS)):
        kernel = kernels[s + 1]
        row = totals[s : s + 1, :]
        column = columns[s][:, 0:1]
        slope = grad[...]
        slope = (slope - jnp.sum(slope * kernel, axis=0, keepdims=True)) / row
        moment = jnp.sum(slope * (kernel * row), axis=1, keepdims=True)
        grad[...] = (slope - moment) / column
    logit_grad = grad[...] * kernels[0]
    weighted = logit_grad * jnp.log(kernels[0])
    turn = logit_grad * (cos_scale * inverse_token) / jnp.sqrt(square)
    spread[:experts, :] = turn
    spread[experts:, :] = jnp.broadcast_to(
        jnp.sum(weighted, axis=0, keepdims=True) * inverse_token * inverse_token,
        (spread.shape[0] - experts, total),
    )

    own_lanes = pl.ds(pl.multiple_of(share * LANES, LANES), LANES)
    features = tok_all[:, :, own_lanes].reshape(total, LANES)
    product = jnp.dot(
        jnp.concatenate(split_three(turn), axis=0), features, preferred_element_type=f32
    )
    product = product[:experts] + product[experts : 2 * experts] + product[2 * experts :]
    own_router = router_ref[:, own_lanes].astype(f32)
    parts[dp] = product - own_router * (jnp.sum(weighted, axis=1, keepdims=True) / square)
    for k, peer in enumerate(x_peers):
        start(copy_of(n + k, parts.at[dp], peer))

    if ring:
        for a in arrays:
            near_plain(a)
        for a in arrays:
            near_joined(a)

    turned[...] = spread[:, pl.ds(pl.multiple_of(me * count // LANES * LANES, LANES), LANES)].T
    own = turned[pl.ds(pl.multiple_of(lax.rem(me, LANES // count) * count, count), count), :]
    back = jnp.zeros((count, width), f32)
    for term in split_three(own[:, :experts]):
        back += jnp.dot(term, router, preferred_element_type=f32)
    back -= tok_ref[...].astype(f32) * own[:, experts : experts + 1]

    for k in range(n_dp - 1):
        copy_of(n + k, parts.at[lax.rem(dp - 1 - k + n_dp, n_dp)], mate).wait_recv()
    n += n_dp - 1
    summed = parts[0]
    for k in range(1, n_dp):
        summed += parts[k]
    shares[share] = summed
    for k, peer in enumerate(share_peers):
        start(copy_of(n + k, shares.at[share], peer))

    def got_rows(k, carry):
        block = lax.rem(me - k + ep, ep)
        row_copy(k, block, block, block).wait_recv()
        return carry

    lax.fori_loop(1, ep, got_rows, 0)
    tokens_out[...] = (
        back
        + jnp.dot(
            slots_ref[...], back_rows[...].reshape(ep * SLOTS, width), preferred_element_type=f32
        )
    ).astype(bf16)

    for k in range(n_shares - 1):
        copy_of(n + k, shares.at[lax.rem(share - 1 - k + n_shares, n_shares)], mate).wait_recv()
    for k in range(n_shares):
        router_out[:, k * LANES : (k + 1) * LANES] = shares[k]

    def finish(a, half):
        value = gradient(a, 0, half)
        if ring:
            for side in range(2):
                near_copy(a, side, half).wait_recv()
                value += got_near[a, side, half].reshape(chunk, hidden_units).astype(f32)
        outs[a][half * chunk : (half + 1) * chunk, :] = value.astype(bf16)

    for a in arrays:
        for half in range(2):
            finish(a, half)

    def sent_rows(k, carry):
        peer = lax.rem(me + k, ep)
        row_copy(k, peer, me, peer).wait_send()
        return carry

    lax.fori_loop(1, ep, sent_rows, 0)
    for copy in started:
        copy.wait_send()


def copy_kernel(*refs):
    arrays = (len(refs) - 2) // 3
    sources, targets, stages = (refs[k * arrays : (k + 1) * arrays] for k in range(3))
    ins = [pltpu.make_async_copy(a, b, refs[-2].at[k]) for k, (a, b) in enumerate(zip(sources, stages))]
    outs = [pltpu.make_async_copy(a, b, refs[-1].at[k]) for k, (a, b) in enumerate(zip(stages, targets))]
    for copy in ins:
        copy.start()
    for arrived, copy in zip(ins, outs):
        arrived.wait()
        copy.start()
    for copy in outs:
        copy.wait()


def handed_on(arrays):
    anywhere = pl.BlockSpec(memory_space=pl.ANY)
    return pl.pallas_call(
        copy_kernel,
        out_shape=tuple(jax.ShapeDtypeStruct(a.shape, a.dtype) for a in arrays),
        in_specs=[anywhere] * len(arrays),
        out_specs=(anywhere,) * len(arrays),
        scratch_shapes=[
            *(pltpu.VMEM(a.shape, a.dtype) for a in arrays),
            pltpu.SemaphoreType.DMA((len(arrays),)),
            pltpu.SemaphoreType.DMA((len(arrays),)),
        ],
    )(*arrays)


def per_device(ep, n_dp, tokens, cotangent, assign, w_router, w_gate, w_up, w_down):
    ny, nz = torus_of(ep)
    _, count, width = tokens.shape
    experts = w_router.shape[1]
    hidden_units = w_gate.shape[2]
    total = ep * count
    groups = total // GROUP
    n_shares = width // LANES
    rows = ep * SLOTS
    chunk = width // n_dp // 2
    copies = 1 + nz - 1 + ny - 1 + n_dp - 1 + n_shares - 1
    blocks = plan_of(ny, nz, width)[1]
    shape, vmem_array, dma = jax.ShapeDtypeStruct, pltpu.VMEM, pltpu.SemaphoreType.DMA
    vmem = pl.BlockSpec(memory_space=pltpu.VMEM)
    anywhere = pl.BlockSpec(memory_space=pl.ANY)
    gradient = shape((2 * chunk, hidden_units), bf16)
    small = nz + ny - 1
    outs = pl.pallas_call(
        functools.partial(moe_kernel, ep, n_dp),
        out_shape=(
            shape((count, width), bf16),
            shape((experts, width), f32),
            gradient,
            gradient,
            gradient,
        ),
        in_specs=[vmem] * 4 + [anywhere] * 3,
        out_specs=(vmem,) * 5,
        scratch_shapes=[
            vmem_array((ep, count, width), bf16),
            vmem_array((ep, count, width), bf16),
            vmem_array((2, ny * nz, count // 2, 2 * experts), f32),
            vmem_array((rows, width), bf16),
            vmem_array((rows, width), bf16),
            vmem_array((rows, 1), f32),
            vmem_array((rows, 1), f32),
            vmem_array((rows, hidden_units), bf16),
            vmem_array((rows, hidden_units), bf16),
            vmem_array((rows, hidden_units), bf16),
            vmem_array((width, hidden_units), bf16),
            vmem_array((width, hidden_units), bf16),
            vmem_array((width, hidden_units), bf16),
            vmem_array((1, total), f32),
            vmem_array((1, total), f32),
            vmem_array((groups, GROUP // count * SLOTS, GROUP), bf16),
            vmem_array((ITERS + 1, experts, total), f32),
            vmem_array((ITERS, experts, LANES), f32),
            vmem_array((8, total), f32),
            vmem_array((experts, total), f32),
            vmem_array((count, experts * SLOTS), bf16),
            vmem_array((rows, hidden_units), f32),
            vmem_array((rows, hidden_units), f32),
            vmem_array((2, chunk // count, count, hidden_units), bf16),
            vmem_array((ny * nz, 2, groups, GROUP), f32),
            vmem_array((experts, total), f32),
            vmem_array((LANES, total), f32),
            vmem_array((LANES, LANES), f32),
            vmem_array((n_dp, experts, LANES), f32),
            vmem_array((n_shares, experts, LANES), f32),
            vmem_array((ep, SLOTS, width), bf16),
            vmem_array((ep, SLOTS, width), bf16),
            vmem_array((3, 2, chunk // count, count, hidden_units), bf16),
            vmem_array((3, 2, 2, chunk // count, count, hidden_units), bf16),
            dma((small,)),
            dma((small,)),
            dma((blocks,)),
            dma((blocks,)),
            dma((copies,)),
            dma((copies,)),
            dma((ep,)),
            dma((ep,)),
            dma((3, 2)),
            dma((3, 2)),
            dma((3, 2, 2)),
            dma((3, 2, 2)),
            dma((3,)),
        ],
        compiler_params=pltpu.CompilerParams(
            collective_id=1, has_side_effects=True, vmem_limit_bytes=60 * 2**20
        ),
    )(tokens[0], cotangent[0], assign[0].T, w_router.T, w_gate[0], w_up[0], w_down[0])
    grad_tokens, grad_router, grad_gate, grad_up, grad_down = handed_on(outs)
    return grad_tokens[None], grad_router.T, grad_gate[None], grad_up[None], grad_down[None]


def solution(mesh):
    return jax.shard_map(
        functools.partial(per_device, mesh.shape["ep"], mesh.shape["dp"]),
        mesh=mesh,
        in_specs=(
            P("dp", "ep", None),
            P("dp", "ep", None),
            P("dp", "ep", None),
            P(),
            P("ep", None, None),
            P("ep", None, None),
            P("ep", None, None),
        ),
        out_specs=(
            P("dp", "ep", None),
            P(),
            P("ep", "dp", None),
            P("ep", "dp", None),
            P("ep", "dp", None),
        ),
        check_vma=False,
    )
```

```python
import functools
import heapq

import jax
import jax.numpy as jnp
from jax import lax
from jax.experimental import pallas as pl
from jax.experimental.pallas import tpu as pltpu
from jax.sharding import PartitionSpec as P

ITERS = 3
SLOTS = 8
LANES = 128
GROUP = 256
MESH = pl.DeviceIdType.MESH
f32 = jnp.float32
bf16 = jnp.bfloat16

cos_scale = 48.0
eps_norm = 1e-06
contract_first = (((0,), (0,)), ((), ()))
contract_last = (((1,), (1,)), ((), ()))


def torus_of(ep):
    ny = max(1, min(4, ep // 4))
    return ny, ep // (2 * ny)


def gather_plan(ny, nz, unit_us, begin_us, hop_us=1.0):
    def half(part, side):
        return side if part is None else (part if part == side else -1)

    def spread(which, a, b, part):
        na, nb = (nz, ny) if which % 2 == 0 else (ny, nz)
        out = []

        def along(axis, n, at, signs):
            for sign in signs:
                last = abs(at) + 1 == n // 2
                piece = half(part, 0 if sign > 0 else 1) if last else part
                if piece != -1:
                    out.append((axis, sign, piece))

        def onward(at, n):
            if n == 1:
                return ()
            if at == 0:
                return (1, -1)
            return ((1,) if at > 0 else (-1,)) if abs(at) < n // 2 else ()

        if b == 0:
            along(0, na, a, onward(a, na))
        along(1, nb, b, onward(b, nb))
        return out

    heap, order, free, steps, ids = [], 0, {}, [], 0
    for which in range(len(unit_us)):
        heapq.heappush(heap, (begin_us[which], order, None, which, 0, 0, None))
        order += 1
    while heap:
        now, _, arrival, which, a, b, part = heapq.heappop(heap)
        dy, dz = (b, a) if which % 2 == 0 else (a, b)
        sends = []
        for axis, sign, piece in spread(which, a, b, part):
            link = "zy"[axis] if which % 2 == 0 else "yz"[axis]
            share = 1.0 if piece is None else 0.5
            end = max(now, free.get((link, sign), 0.0)) + unit_us[which] * share
            free[(link, sign)] = end
            na, nb = (a + sign, b) if axis == 0 else (a, b + sign)
            heapq.heappush(heap, (end + hop_us, order, ids, which, na, nb, piece))
            sends.append((ids, which, dy, dz, part if piece is None else piece, link, sign))
            order += 1
            ids += 1
        sends.append((ids, which, dy, dz, part, "mate", 0))
        ids += 1
        steps.append((None if arrival is None else (arrival, which, dy, dz, part), sends))
    return steps, ids


def pieces_of(width):
    split = width * 5 // 8 // LANES * LANES
    return tuple(
        (held, column, columns)
        for held in (0, 1)
        for column, columns in ((0, split), (split, width - split))
    )


def plan_of(ny, nz, width):
    times = tuple(2.8 * columns / width for _, _, columns in pieces_of(width))
    return gather_plan(ny, nz, times, (0.0, 0.0, 14.0, 14.0))


def place(ep, ny, nz):
    me = lax.axis_index("ep")
    core = lax.rem(me, 2)
    chip = me // 2
    return me, core, chip // nz, lax.rem(chip, nz)


def at_ep(nz, y, z, core):
    return (y * nz + z) * 2 + core


def split_three(value):
    high = value.astype(bf16)
    rest = value - high.astype(f32)
    middle = rest.astype(bf16)
    return high, middle, (rest - middle.astype(f32)).astype(bf16)


def balance(meta, kernels, columns, totals, marks, per_group):
    experts, total = marks.shape
    for g in range(total // GROUP):
        blocks = []
        for b in range(g * per_group, (g + 1) * per_group):
            block = meta[b % 2, b // 2]
            blocks += [block[:, :experts], block[:, experts:]]
        flipped = jnp.concatenate(blocks, axis=0).T
        marks[:, g * GROUP : (g + 1) * GROUP] = flipped
    kernels[0] = jnp.abs(marks[...])
    for s in range(ITERS):
        kernel = kernels[s]
        column = jnp.sum(kernel, axis=1, keepdims=True)
        scaled = kernel / column
        row = jnp.sum(scaled, axis=0, keepdims=True)
        kernels[s + 1] = scaled / row
        columns[s] = jnp.broadcast_to(column, (experts, LANES))
        totals[s : s + 1, :] = row
    picked = jnp.where(marks[...] < 0.0, kernels[ITERS], 0.0)
    totals[ITERS : ITERS + 1, :] = jnp.sum(picked, axis=0, keepdims=True)


def moe_kernel(
    ep,
    n_dp,
    tok_ref,
    cot_ref,
    assign_ref,
    router_ref,
    w_gate_hbm,
    w_up_hbm,
    w_down_hbm,
    tokens_out,
    router_out,
    gate_out,
    up_out,
    down_out,
    tok_all,
    cot_all,
    meta,
    rows_tok,
    rows_cot,
    rows_gate,
    gate_grad,
    gate_delta,
    up_delta,
    weighted_rows,
    w_gate,
    w_up,
    w_down,
    row_mask,
    row_gate,
    pick,
    kernels,
    columns,
    totals,
    marks,
    slots_ref,
    gate_all,
    up_all,
    spare,
    table,
    grad,
    spread,
    turned,
    parts,
    shares,
    route_back,
    back_rows,
    got_far,
    got_near,
    meta_send,
    meta_recv,
    block_sends,
    block_recvs,
    sends,
    recvs,
    row_sends,
    row_recvs,
    far_sends,
    far_recvs,
    near_sends,
    near_recvs,
    weight_sems,
):
    ny, nz = torus_of(ep)
    count, width = tok_ref.shape
    experts = router_ref.shape[0]
    hidden_units = gate_delta.shape[1]
    total = ep * count
    groups = total // GROUP
    per_group = GROUP // count
    slots = per_group * SLOTS
    n_shares = width // LANES
    repeat = ep // n_shares
    chunk = width // n_dp // 2
    chunk_blocks = chunk // count
    ring = n_dp == 4
    dp = lax.axis_index("dp")
    me, core, y, z = place(ep, ny, nz)
    mine = y * nz + z
    mate = (dp, at_ep(nz, y, z, 1 - core))
    z_peers = [(dp, at_ep(nz, y, lax.rem(z + k, nz), core)) for k in range(1, nz)]
    y_peers = [(dp, at_ep(nz, lax.rem(y + k, ny), z, core)) for k in range(1, ny)]
    x_peers = [(lax.rem(dp + k, n_dp), me) for k in range(1, n_dp)]
    right, left = (lax.rem(dp + 1, n_dp), me), (lax.rem(dp + n_dp - 1, n_dp), me)
    share, twin = me // repeat, lax.rem(me, repeat)
    share_peers = [
        (dp, lax.rem(share + k, n_shares) * repeat + twin) for k in range(1, n_shares)
    ]

    barrier = pltpu.get_barrier_semaphore()

    def greet(k, carry):
        pl.semaphore_signal(
            barrier, inc=1, device_id=(dp, lax.rem(me + k, ep)), device_id_type=MESH
        )
        return carry

    lax.fori_loop(1, ep, greet, 0)
    for peer in x_peers:
        pl.semaphore_signal(barrier, inc=1, device_id=peer, device_id_type=MESH)
    fetches = [
        pltpu.make_async_copy(source, target, weight_sems.at[k])
        for k, (source, target) in enumerate(
            ((w_gate_hbm, w_gate), (w_up_hbm, w_up), (w_down_hbm, w_down))
        )
    ]
    for fetch in fetches:
        fetch.start()

    local = tok_ref[...]
    router = router_ref[...]
    tok_all[me] = local
    cot_all[me] = cot_ref[...]
    wide = local.astype(f32)
    inverse_local = 1.0 / jnp.sqrt(jnp.sum(wide * wide, axis=1, keepdims=True) + eps_norm)
    router_wide = router.astype(f32)
    square = jnp.sum(router_wide * router_wide, axis=1, keepdims=True) + eps_norm
    square_row = jnp.broadcast_to(square, (experts, LANES)).T[0:1, :]
    inner = lax.dot_general(local, router, contract_last, preferred_element_type=f32)
    logits = cos_scale * inner * inverse_local / jnp.sqrt(square_row)
    ids = lax.broadcasted_iota(jnp.int32, (count, experts), 1).astype(f32)
    routes = assign_ref[...].astype(f32).T
    named = jnp.zeros((count, experts), f32)
    for k in range(routes.shape[1]):
        named = jnp.where(routes[:, k : k + 1] == ids, 1.0, named)
    start_kernel = jnp.exp(logits)
    signed = jnp.where(named > 0.0, -start_kernel, start_kernel)
    meta[core, mine] = jnp.concatenate([signed[: count // 2], signed[count // 2 :]], axis=1)

    pl.semaphore_wait(barrier, ep - 1 + n_dp - 1)

    def meta_copy(n, block, blocks, peer, c=core):
        ref = meta.at[c, pl.ds(block, blocks)]
        return pltpu.make_async_remote_copy(
            src_ref=ref, dst_ref=ref, send_sem=meta_send.at[n], recv_sem=meta_recv.at[n],
            device_id=peer, device_id_type=MESH,
        )

    meta_copies = [meta_copy(k, mine, 1, p) for k, p in enumerate(z_peers)]
    for copy in meta_copies:
        copy.start()

    ends = {
        ("z", 1): (dp, at_ep(nz, y, lax.rem(z + 1, nz), core)),
        ("z", -1): (dp, at_ep(nz, y, lax.rem(z + nz - 1, nz), core)),
        ("y", 1): (dp, at_ep(nz, lax.rem(y + 1, ny), z, core)),
        ("y", -1): (dp, at_ep(nz, lax.rem(y + ny - 1, ny), z, core)),
        ("mate", 0): mate,
    }

    def view(which, dy, dz, part, c):
        block = at_ep(nz, lax.rem(y - dy + 2 * ny, ny), lax.rem(z - dz + 2 * nz, nz), c)
        first, rows = (0, count) if part is None else (part * (count // 2), count // 2)
        ref, column, columns_held = pieces_of(width)[which]
        held = (tok_all, cot_all)[ref]
        return held.at[block, pl.ds(first, rows), pl.ds(column, columns_held)]

    def block_copy(n, ref, end):
        return pltpu.make_async_remote_copy(
            src_ref=ref, dst_ref=ref, send_sem=block_sends.at[n], recv_sem=block_recvs.at[n],
            device_id=ends[end], device_id_type=MESH,
        )

    gather_copies, mate_arrivals = [], []

    def run(step):
        arrival, step_sends = step
        if arrival is not None:
            n, which, dy, dz, part = arrival
            block_copy(n, view(which, dy, dz, part, core), ("z", 1)).wait_recv()
        for n, which, dy, dz, part, link, sign in step_sends:
            copy = block_copy(n, view(which, dy, dz, part, core), (link, sign))
            copy.start()
            gather_copies.append(copy)
            if link == "mate":
                mate_arrivals.append((n, which, dy, dz, part))

    steps = plan_of(ny, nz, width)[0]

    def compact(held, rows_ref, g):
        blocks = held[g * per_group : (g + 1) * per_group].reshape(GROUP, width)
        rows_ref[g * slots : (g + 1) * slots, :] = jnp.dot(
            pick[g], blocks, preferred_element_type=f32
        ).astype(bf16)

    row_step = min(256, ep * SLOTS)
    unit_step = min(256, hidden_units)
    row_steps = ep * SLOTS // row_step
    expert_steps = row_steps * (hidden_units // unit_step)

    def tile(i):
        row, unit = i % row_steps * row_step, i // row_steps * unit_step
        return slice(row, row + row_step), slice(unit, unit + unit_step)

    def forward(i):
        rows, units = tile(i)
        gate_linear = jnp.dot(rows_tok[rows, :], w_gate[:, units], preferred_element_type=f32)
        up_linear = jnp.dot(rows_tok[rows, :], w_up[:, units], preferred_element_type=f32)
        gate_all[rows, units] = gate_linear
        up_all[rows, units] = up_linear
        product = gate_linear * jax.nn.sigmoid(gate_linear) * up_linear
        weighted_rows[rows, units] = (rows_gate[rows, :] * product).astype(bf16)

    def norms(g):
        values = tok_all[g * per_group : (g + 1) * per_group].reshape(GROUP, width).astype(f32)
        inverse = 1.0 / jnp.sqrt(jnp.sum(values * values, axis=1, keepdims=True) + eps_norm)
        totals[ITERS + 1 : ITERS + 2, g * GROUP : (g + 1) * GROUP] = jnp.broadcast_to(
            inverse, (GROUP, LANES)
        ).T[0:1, :]

    def mates(wanted):
        for n, which, dy, dz, part in mate_arrivals:
            if pieces_of(width)[which][0] == wanted:
                block_copy(n, view(which, dy, dz, part, 1 - core), ("mate", 0)).wait_recv()

    def fetched():
        for fetch in fetches:
            fetch.wait()

    token_work = [functools.partial(compact, tok_all, rows_tok, g) for g in range(groups)]
    token_work += [fetched]
    token_work += [functools.partial(forward, i) for i in range(expert_steps)]
    token_work += [functools.partial(norms, g) for g in range(groups)]
    all_work = len(token_work)
    tokens_in = max(
        at for at, step in enumerate(steps) if pieces_of(width)[step[0][1] if step[0] else 0][0] == 0
    )
    first, second = tokens_in // 6, tokens_in // 3
    third, fourth = tokens_in // 2, tokens_in * 2 // 3
    ready = min(tokens_in + 4, len(steps) - 1)
    for at, step in enumerate(steps):
        if at == first:
            for k in range(nz - 1):
                meta_copy(k, y * nz + lax.rem(z - 1 - k + nz, nz), 1, mate).wait_recv()
            for k, peer in enumerate(y_peers):
                meta_copies.append(meta_copy(nz - 1 + k, y * nz, nz, peer))
                meta_copies[-1].start()
        if at == second:
            for k in range(ny - 1):
                block = lax.rem(y - 1 - k + ny, ny) * nz
                meta_copy(nz - 1 + k, block, nz, mate).wait_recv()
            meta_copies.append(meta_copy(nz + ny - 2, 0, ny * nz, mate))
            meta_copies[-1].start()
        if at == third:
            meta_copy(nz + ny - 2, 0, ny * nz, mate, 1 - core).wait_recv()
            tokens_down = lax.broadcasted_iota(jnp.int32, (count, count), 0)
            tokens_across = lax.broadcasted_iota(jnp.int32, (count, count), 1)
            sooner = jnp.where(tokens_across < tokens_down, 1.0, 0.0).astype(bf16)
            rank = jnp.dot(sooner, named.astype(bf16), preferred_element_type=f32)
            slot_of = jnp.where(named > 0.0, rank, -1.0).astype(bf16)
            expert_down = lax.broadcasted_iota(jnp.int32, (experts, experts * SLOTS), 0)
            slot_across = lax.broadcasted_iota(jnp.int32, (experts, experts * SLOTS), 1)
            widen = jnp.where(slot_across // SLOTS == expert_down, 1.0, 0.0).astype(bf16)
            slot_wide = jnp.dot(slot_of, widen, preferred_element_type=f32)
            across = lax.broadcasted_iota(jnp.int32, (count, experts * SLOTS), 1)
            slots_ref[...] = jnp.where(
                slot_wide == lax.rem(across, SLOTS).astype(f32), 1.0, 0.0
            ).astype(bf16)
        if at == fourth:
            balance(meta, kernels, columns, totals, marks, per_group)
            held = marks[pl.ds(me, 1), :] < 0.0
            kernel = jnp.where(held, kernels[ITERS, pl.ds(me, 1), :], 0.0)
            row_mask[...] = jnp.where(held, 1.0, 0.0)
            row_gate[...] = (kernel / totals[ITERS : ITERS + 1, :]).astype(bf16).astype(f32)
            before = lax.broadcasted_iota(jnp.int32, (GROUP, GROUP), 0)
            after = lax.broadcasted_iota(jnp.int32, (GROUP, GROUP), 1)
            earlier = jnp.where(
                (before < after) & (before // count == after // count), 1.0, 0.0
            ).astype(bf16)
            slot_ids = lax.broadcasted_iota(jnp.int32, (slots, GROUP), 0).astype(f32)
            base = (lax.broadcasted_iota(jnp.int32, (1, GROUP), 1) // count * SLOTS).astype(f32)
            for g in range(groups):
                mask = row_mask[:, g * GROUP : (g + 1) * GROUP]
                place_in = jnp.dot(
                    jnp.broadcast_to(mask, (8, GROUP)).astype(bf16), earlier,
                    preferred_element_type=f32,
                )[0:1]
                target = jnp.where(mask > 0.0, base + place_in, -1.0)
                chosen = jnp.where(slot_ids == target, 1.0, 0.0)
                rows_gate[g * slots : (g + 1) * slots, :] = jnp.sum(
                    chosen * row_gate[:, g * GROUP : (g + 1) * GROUP], axis=1, keepdims=True
                )
                pick[g] = chosen.astype(bf16)
        if at == ready:
            mates(0)
        if at > ready:
            done = all_work - len(token_work)
            due = all_work * (at - ready) // (len(steps) - 1 - ready) - done
            for work in token_work[:due]:
                work()
            token_work = token_work[due:]
        run(step)
    for work in token_work:
        work()
    mates(1)
    for g in range(groups):
        compact(cot_all, rows_cot, g)

    started = []
    across_table = width // hidden_units

    def buffer(n):
        if n < 2:
            return spare.at[n]
        block, column = (n - 2) // across_table, (n - 2) % across_table
        return cot_all.at[
            pl.ds(block * chunk_blocks, chunk_blocks),
            :,
            pl.ds(column * hidden_units, hidden_units),
        ]

    def far_buffer(a, side):
        return buffer(a * 2 + side)

    def near_buffer(a, side, half):
        return buffer(6 + a * 4 + side * 2 + half)

    def copy_of(n, ref, peer):
        return pltpu.make_async_remote_copy(
            src_ref=ref, dst_ref=ref, send_sem=sends.at[n], recv_sem=recvs.at[n],
            device_id=peer, device_id_type=MESH,
        )

    def start(copy):
        copy.start()
        started.append(copy)

    def far_copy(a, side):
        return pltpu.make_async_remote_copy(
            src_ref=far_buffer(a, side), dst_ref=got_far.at[a, side],
            send_sem=far_sends.at[a, side], recv_sem=far_recvs.at[a, side],
            device_id=(right, left)[side], device_id_type=MESH,
        )

    def near_copy(a, side, half):
        return pltpu.make_async_remote_copy(
            src_ref=near_buffer(a, side, half), dst_ref=got_near.at[a, side, half],
            send_sem=near_sends.at[a, side, half], recv_sem=near_recvs.at[a, side, half],
            device_id=(right, left)[side], device_id_type=MESH,
        )

    pairs = ((rows_cot, weighted_rows), (rows_tok, up_delta), (rows_tok, gate_delta))
    outs = (down_out, up_out, gate_out)
    arrays = range(3)

    def gradient(a, away, half):
        block = lax.rem(dp + away, n_dp)
        start_row = pl.multiple_of(block * (2 * chunk) + half * chunk, chunk)
        left_rows, right_rows = pairs[a]
        return lax.dot_general(
            left_rows[:, pl.ds(start_row, chunk)], right_rows[...], contract_first,
            preferred_element_type=f32,
        )

    def put(ref, value):
        ref[...] = value.astype(bf16).reshape(chunk_blocks, count, hidden_units)

    def far(a):
        for side in range(2):
            put(far_buffer(a, side), gradient(a, 2, side))
            start(far_copy(a, side))

    def near_plain(a):
        for side in range(2):
            put(near_buffer(a, side, 1 - side), gradient(a, (1, n_dp - 1)[side], 1 - side))
            start(near_copy(a, side, 1 - side))

    def near_joined(a):
        for side in range(2):
            mixed = gradient(a, (1, n_dp - 1)[side], side)
            far_copy(a, side).wait_recv()
            put(
                near_buffer(a, side, side),
                mixed + got_far[a, side].reshape(chunk, hidden_units).astype(f32),
            )
            start(near_copy(a, side, side))

    if ring:
        far(0)

    gate_grad[...] = jnp.zeros_like(gate_grad)

    def expert(i, carry):
        rows = pl.ds(pl.multiple_of(lax.rem(i, row_steps) * row_step, row_step), row_step)
        units = pl.ds(pl.multiple_of(i // row_steps * unit_step, unit_step), unit_step)
        raw_back = jnp.dot(rows_cot[rows, :], w_down[:, units], preferred_element_type=f32)
        gate_linear = gate_all[rows, units]
        up_linear = up_all[rows, units]
        sigmoid_gate = jax.nn.sigmoid(gate_linear)
        activation = gate_linear * sigmoid_gate
        product = activation * up_linear
        gate_grad[rows, :] += jnp.sum(
            raw_back * product.astype(bf16).astype(f32), axis=1, keepdims=True
        )
        scaled_back = rows_gate[rows, :] * raw_back
        up_delta[rows, units] = (scaled_back * activation).astype(bf16)
        gate_delta[rows, units] = (
            scaled_back * up_linear * sigmoid_gate * (1.0 + gate_linear * (1.0 - sigmoid_gate))
        ).astype(bf16)
        return carry

    lax.fori_loop(0, expert_steps, expert, 0)
    for copy in [*meta_copies, *gather_copies]:
        copy.wait_send()

    for g in range(groups):
        held = gate_grad[g * slots : (g + 1) * slots, :].astype(bf16).astype(f32)
        table[mine, core, g : g + 1, :] = jnp.sum(
            held * pick[g].astype(f32), axis=0, keepdims=True
        )
    n = 0

    def part(chip, chips):
        return table.at[pl.ds(chip, chips)]

    start(copy_of(n, table.at[mine, core], mate))
    if ring:
        far(1)
    copy_of(n, table.at[mine, 1 - core], mate).wait_recv()
    n += 1
    for k, peer in enumerate(z_peers):
        start(copy_of(n + k, part(mine, 1), peer))
    if ring:
        far(2)
    for k in range(nz - 1):
        copy_of(n + k, part(y * nz + lax.rem(z - 1 - k + nz, nz), 1), mate).wait_recv()
    n += nz - 1
    for k, peer in enumerate(y_peers):
        start(copy_of(n + k, part(y * nz, nz), peer))

    pieces = 4
    rows_each = ep // pieces

    def rows_back(q, carry):
        rows = pl.ds(pl.multiple_of(q * rows_each * SLOTS, rows_each * SLOTS), rows_each * SLOTS)
        value = lax.dot_general(
            gate_delta[rows, :], w_gate[...], contract_last, preferred_element_type=f32
        ) + lax.dot_general(up_delta[rows, :], w_up[...], contract_last, preferred_element_type=f32)
        route_back[pl.ds(q * rows_each, rows_each)] = value.astype(bf16).reshape(
            rows_each, SLOTS, width
        )
        return carry

    lax.fori_loop(0, pieces, rows_back, 0)

    def row_copy(k, from_block, to_block, peer):
        return pltpu.make_async_remote_copy(
            src_ref=route_back.at[from_block], dst_ref=back_rows.at[to_block],
            send_sem=row_sends.at[k], recv_sem=row_recvs.at[k],
            device_id=(dp, peer), device_id_type=MESH,
        )

    def send_rows(k, carry):
        peer = lax.rem(me + k, ep)
        row_copy(k, peer, me, peer).start()
        return carry

    lax.fori_loop(1, ep, send_rows, 0)
    back_rows[me] = route_back[me]
    if ring:
        near_plain(0)

    for k in range(ny - 1):
        copy_of(n + k, part(lax.rem(y - 1 - k + ny, ny) * nz, nz), mate).wait_recv()
    n += ny - 1

    for g in range(groups):
        both = table[:, :, g, :]
        grad[:, g * GROUP : (g + 1) * GROUP] = both.reshape(experts, GROUP)
    inverse_token = totals[ITERS + 1 : ITERS + 2, :]
    picked_sum = totals[ITERS : ITERS + 1, :]
    member = marks[...] < 0.0
    route = jnp.where(member, grad[...], 0.0)
    gates = jnp.where(member, kernels[ITERS], 0.0) / picked_sum
    grad[...] = jnp.where(
        member, (route - jnp.sum(route * gates, axis=0, keepdims=True)) / picked_sum, 0.0
    )
    for s in reversed(range(ITERS)):
        kernel = kernels[s + 1]
        row = totals[s : s + 1, :]
        column = columns[s][:, 0:1]
        slope = grad[...]
        slope = (slope - jnp.sum(slope * kernel, axis=0, keepdims=True)) / row
        moment = jnp.sum(slope * (kernel * row), axis=1, keepdims=True)
        grad[...] = (slope - moment) / column
    logit_grad = grad[...] * kernels[0]
    weighted = logit_grad * jnp.log(kernels[0])
    turn = logit_grad * (cos_scale * inverse_token) / jnp.sqrt(square)
    spread[:experts, :] = turn
    spread[experts:, :] = jnp.broadcast_to(
        jnp.sum(weighted, axis=0, keepdims=True) * inverse_token * inverse_token,
        (spread.shape[0] - experts, total),
    )

    own_lanes = pl.ds(pl.multiple_of(share * LANES, LANES), LANES)
    features = tok_all[:, :, own_lanes].reshape(total, LANES)
    product = jnp.dot(
        jnp.concatenate(split_three(turn), axis=0), features, preferred_element_type=f32
    )
    product = product[:experts] + product[experts : 2 * experts] + product[2 * experts :]
    own_router = router_ref[:, own_lanes].astype(f32)
    parts[dp] = product - own_router * (jnp.sum(weighted, axis=1, keepdims=True) / square)
    for k, peer in enumerate(x_peers):
        start(copy_of(n + k, parts.at[dp], peer))

    if ring:
        for a in (1, 2):
            near_plain(a)
        for a in arrays:
            near_joined(a)

    turned[...] = spread[:, pl.ds(pl.multiple_of(me * count // LANES * LANES, LANES), LANES)].T
    own = turned[pl.ds(pl.multiple_of(lax.rem(me, LANES // count) * count, count), count), :]
    back = jnp.zeros((count, width), f32)
    for term in split_three(own[:, :experts]):
        back += jnp.dot(term, router, preferred_element_type=f32)
    back -= tok_ref[...].astype(f32) * own[:, experts : experts + 1]

    for k in range(n_dp - 1):
        copy_of(n + k, parts.at[lax.rem(dp - 1 - k + n_dp, n_dp)], mate).wait_recv()
    n += n_dp - 1
    summed = parts[0]
    for k in range(1, n_dp):
        summed += parts[k]
    shares[share] = summed
    for k, peer in enumerate(share_peers):
        start(copy_of(n + k, shares.at[share], peer))

    def got_rows(k, carry):
        block = lax.rem(me - k + ep, ep)
        row_copy(k, block, block, block).wait_recv()
        return carry

    lax.fori_loop(1, ep, got_rows, 0)
    tokens_out[...] = (
        back
        + jnp.dot(
            slots_ref[...], back_rows[...].reshape(ep * SLOTS, width), preferred_element_type=f32
        )
    ).astype(bf16)

    for k in range(n_shares - 1):
        copy_of(n + k, shares.at[lax.rem(share - 1 - k + n_shares, n_shares)], mate).wait_recv()
    for k in range(n_shares):
        router_out[:, k * LANES : (k + 1) * LANES] = shares[k]

    def finish(a, half):
        value = gradient(a, 0, half)
        if ring:
            for side in range(2):
                near_copy(a, side, half).wait_recv()
                value += got_near[a, side, half].reshape(chunk, hidden_units).astype(f32)
        outs[a][half * chunk : (half + 1) * chunk, :] = value.astype(bf16)

    for a in arrays:
        for half in range(2):
            finish(a, half)

    def sent_rows(k, carry):
        peer = lax.rem(me + k, ep)
        row_copy(k, peer, me, peer).wait_send()
        return carry

    lax.fori_loop(1, ep, sent_rows, 0)
    for copy in started:
        copy.wait_send()


def copy_kernel(*refs):
    arrays = (len(refs) - 2) // 3
    sources, targets, stages = (refs[k * arrays : (k + 1) * arrays] for k in range(3))
    ins = [pltpu.make_async_copy(a, b, refs[-2].at[k]) for k, (a, b) in enumerate(zip(sources, stages))]
    outs = [pltpu.make_async_copy(a, b, refs[-1].at[k]) for k, (a, b) in enumerate(zip(stages, targets))]
    for copy in ins:
        copy.start()
    for arrived, copy in zip(ins, outs):
        arrived.wait()
        copy.start()
    for copy in outs:
        copy.wait()


def handed_on(arrays):
    anywhere = pl.BlockSpec(memory_space=pl.ANY)
    return pl.pallas_call(
        copy_kernel,
        out_shape=tuple(jax.ShapeDtypeStruct(a.shape, a.dtype) for a in arrays),
        in_specs=[anywhere] * len(arrays),
        out_specs=(anywhere,) * len(arrays),
        scratch_shapes=[
            *(pltpu.VMEM(a.shape, a.dtype) for a in arrays),
            pltpu.SemaphoreType.DMA((len(arrays),)),
            pltpu.SemaphoreType.DMA((len(arrays),)),
        ],
    )(*arrays)


def per_device(ep, n_dp, tokens, cotangent, assign, w_router, w_gate, w_up, w_down):
    ny, nz = torus_of(ep)
    _, count, width = tokens.shape
    experts = w_router.shape[1]
    hidden_units = w_gate.shape[2]
    total = ep * count
    groups = total // GROUP
    n_shares = width // LANES
    rows = ep * SLOTS
    chunk = width // n_dp // 2
    copies = 1 + nz - 1 + ny - 1 + n_dp - 1 + n_shares - 1
    blocks = plan_of(ny, nz, width)[1]
    shape, vmem_array, dma = jax.ShapeDtypeStruct, pltpu.VMEM, pltpu.SemaphoreType.DMA
    vmem = pl.BlockSpec(memory_space=pltpu.VMEM)
    anywhere = pl.BlockSpec(memory_space=pl.ANY)
    gradient = shape((2 * chunk, hidden_units), bf16)
    small = nz + ny - 1
    outs = pl.pallas_call(
        functools.partial(moe_kernel, ep, n_dp),
        out_shape=(
            shape((count, width), bf16),
            shape((experts, width), f32),
            gradient,
            gradient,
            gradient,
        ),
        in_specs=[vmem] * 4 + [anywhere] * 3,
        out_specs=(vmem,) * 5,
        scratch_shapes=[
            vmem_array((ep, count, width), bf16),
            vmem_array((ep, count, width), bf16),
            vmem_array((2, ny * nz, count // 2, 2 * experts), f32),
            vmem_array((rows, width), bf16),
            vmem_array((rows, width), bf16),
            vmem_array((rows, 1), f32),
            vmem_array((rows, 1), f32),
            vmem_array((rows, hidden_units), bf16),
            vmem_array((rows, hidden_units), bf16),
            vmem_array((rows, hidden_units), bf16),
            vmem_array((width, hidden_units), bf16),
            vmem_array((width, hidden_units), bf16),
            vmem_array((width, hidden_units), bf16),
            vmem_array((1, total), f32),
            vmem_array((1, total), f32),
            vmem_array((groups, GROUP // count * SLOTS, GROUP), bf16),
            vmem_array((ITERS + 1, experts, total), f32),
            vmem_array((ITERS, experts, LANES), f32),
            vmem_array((8, total), f32),
            vmem_array((experts, total), f32),
            vmem_array((count, experts * SLOTS), bf16),
            vmem_array((rows, hidden_units), f32),
            vmem_array((rows, hidden_units), f32),
            vmem_array((2, chunk // count, count, hidden_units), bf16),
            vmem_array((ny * nz, 2, groups, GROUP), f32),
            vmem_array((experts, total), f32),
            vmem_array((LANES, total), f32),
            vmem_array((LANES, LANES), f32),
            vmem_array((n_dp, experts, LANES), f32),
            vmem_array((n_shares, experts, LANES), f32),
            vmem_array((ep, SLOTS, width), bf16),
            vmem_array((ep, SLOTS, width), bf16),
            vmem_array((3, 2, chunk // count, count, hidden_units), bf16),
            vmem_array((3, 2, 2, chunk // count, count, hidden_units), bf16),
            dma((small,)),
            dma((small,)),
            dma((blocks,)),
            dma((blocks,)),
            dma((copies,)),
            dma((copies,)),
            dma((ep,)),
            dma((ep,)),
            dma((3, 2)),
            dma((3, 2)),
            dma((3, 2, 2)),
            dma((3, 2, 2)),
            dma((3,)),
        ],
        compiler_params=pltpu.CompilerParams(
            collective_id=1, has_side_effects=True, vmem_limit_bytes=60 * 2**20
        ),
    )(tokens[0], cotangent[0], assign[0].T, w_router.T, w_gate[0], w_up[0], w_down[0])
    grad_tokens, grad_router, grad_gate, grad_up, grad_down = handed_on(outs)
    return grad_tokens[None], grad_router.T, grad_gate[None], grad_up[None], grad_down[None]


def solution(mesh):
    return jax.shard_map(
        functools.partial(per_device, mesh.shape["ep"], mesh.shape["dp"]),
        mesh=mesh,
        in_specs=(
            P("dp", "ep", None),
            P("dp", "ep", None),
            P("dp", "ep", None),
            P(),
            P("ep", None, None),
            P("ep", None, None),
            P("ep", None, None),
        ),
        out_specs=(
            P("dp", "ep", None),
            P(),
            P("ep", "dp", None),
            P("ep", "dp", None),
            P("ep", "dp", None),
        ),
        check_vma=False,
    )
```

```python
import functools
import heapq

import jax
import jax.numpy as jnp
from jax import lax
from jax.experimental import pallas as pl
from jax.experimental.pallas import tpu as pltpu
from jax.sharding import PartitionSpec as P

ITERS = 3
SLOTS = 8
LANES = 128
GROUP = 256
MESH = pl.DeviceIdType.MESH
f32 = jnp.float32
bf16 = jnp.bfloat16

cos_scale = 48.0
eps_norm = 1e-06
contract_first = (((0,), (0,)), ((), ()))
contract_last = (((1,), (1,)), ((), ()))


def torus_of(ep):
    ny = max(1, min(4, ep // 4))
    return ny, ep // (2 * ny)


def gather_plan(ny, nz, unit_us, begin_us, hop_us=1.0):
    def half(part, side):
        return side if part is None else (part if part == side else -1)

    def spread(which, a, b, part):
        na, nb = (nz, ny) if which % 2 == 0 else (ny, nz)
        out = []

        def along(axis, n, at, signs):
            for sign in signs:
                last = abs(at) + 1 == n // 2
                piece = half(part, 0 if sign > 0 else 1) if last else part
                if piece != -1:
                    out.append((axis, sign, piece))

        def onward(at, n):
            if n == 1:
                return ()
            if at == 0:
                return (1, -1)
            return ((1,) if at > 0 else (-1,)) if abs(at) < n // 2 else ()

        if b == 0:
            along(0, na, a, onward(a, na))
        along(1, nb, b, onward(b, nb))
        return out

    heap, order, free, steps, ids = [], 0, {}, [], 0
    for which in range(len(unit_us)):
        heapq.heappush(heap, (begin_us[which], order, None, which, 0, 0, None))
        order += 1
    while heap:
        now, _, arrival, which, a, b, part = heapq.heappop(heap)
        dy, dz = (b, a) if which % 2 == 0 else (a, b)
        sends = []
        for axis, sign, piece in spread(which, a, b, part):
            link = "zy"[axis] if which % 2 == 0 else "yz"[axis]
            share = 1.0 if piece is None else 0.5
            end = max(now, free.get((link, sign), 0.0)) + unit_us[which] * share
            free[(link, sign)] = end
            na, nb = (a + sign, b) if axis == 0 else (a, b + sign)
            heapq.heappush(heap, (end + hop_us, order, ids, which, na, nb, piece))
            sends.append((ids, which, dy, dz, part if piece is None else piece, link, sign))
            order += 1
            ids += 1
        sends.append((ids, which, dy, dz, part, "mate", 0))
        ids += 1
        steps.append((None if arrival is None else (arrival, which, dy, dz, part), sends))
    return steps, ids


def pieces_of(width):
    split = width * 5 // 8 // LANES * LANES
    return tuple(
        (held, column, columns)
        for held in (0, 1)
        for column, columns in ((0, split), (split, width - split))
    )


def plan_of(ny, nz, width):
    times = tuple(2.8 * columns / width for _, _, columns in pieces_of(width))
    return gather_plan(ny, nz, times, (0.0, 0.0, 14.0, 14.0))


def place(ep, ny, nz):
    me = lax.axis_index("ep")
    core = lax.rem(me, 2)
    chip = me // 2
    return me, core, chip // nz, lax.rem(chip, nz)


def at_ep(nz, y, z, core):
    return (y * nz + z) * 2 + core


def split_three(value):
    high = value.astype(bf16)
    rest = value - high.astype(f32)
    middle = rest.astype(bf16)
    return high, middle, (rest - middle.astype(f32)).astype(bf16)


def balance(meta, kernels, columns, totals, marks, per_group):
    experts, total = marks.shape
    for g in range(total // GROUP):
        blocks = []
        for b in range(g * per_group, (g + 1) * per_group):
            block = meta[b % 2, b // 2]
            blocks += [block[:, :experts], block[:, experts:]]
        flipped = jnp.concatenate(blocks, axis=0).T
        marks[:, g * GROUP : (g + 1) * GROUP] = flipped
    kernels[0] = jnp.abs(marks[...])
    for s in range(ITERS):
        kernel = kernels[s]
        column = jnp.sum(kernel, axis=1, keepdims=True)
        scaled = kernel / column
        row = jnp.sum(scaled, axis=0, keepdims=True)
        kernels[s + 1] = scaled / row
        columns[s] = jnp.broadcast_to(column, (experts, LANES))
        totals[s : s + 1, :] = row
    picked = jnp.where(marks[...] < 0.0, kernels[ITERS], 0.0)
    totals[ITERS : ITERS + 1, :] = jnp.sum(picked, axis=0, keepdims=True)


def moe_kernel(
    ep,
    n_dp,
    tok_ref,
    cot_ref,
    assign_ref,
    router_ref,
    w_gate_hbm,
    w_up_hbm,
    w_down_hbm,
    tokens_out,
    router_out,
    gate_out,
    up_out,
    down_out,
    tok_all,
    cot_all,
    meta,
    rows_tok,
    rows_cot,
    rows_gate,
    gate_grad,
    gate_delta,
    up_delta,
    weighted_rows,
    w_gate,
    w_up,
    w_down,
    row_mask,
    row_gate,
    pick,
    kernels,
    columns,
    totals,
    marks,
    slots_ref,
    gate_all,
    up_all,
    spare,
    staged,
    table,
    grad,
    spread,
    turned,
    parts,
    shares,
    route_back,
    back_rows,
    got_far,
    got_near,
    meta_send,
    meta_recv,
    block_sends,
    block_recvs,
    sends,
    recvs,
    row_sends,
    row_recvs,
    far_sends,
    far_recvs,
    near_sends,
    near_recvs,
    weight_sems,
    out_sems,
):
    ny, nz = torus_of(ep)
    count, width = tok_ref.shape
    experts = router_ref.shape[0]
    hidden_units = gate_delta.shape[1]
    total = ep * count
    groups = total // GROUP
    per_group = GROUP // count
    slots = per_group * SLOTS
    n_shares = width // LANES
    repeat = ep // n_shares
    chunk = width // n_dp // 2
    chunk_blocks = chunk // count
    ring = n_dp == 4
    dp = lax.axis_index("dp")
    me, core, y, z = place(ep, ny, nz)
    mine = y * nz + z
    mate = (dp, at_ep(nz, y, z, 1 - core))
    z_peers = [(dp, at_ep(nz, y, lax.rem(z + k, nz), core)) for k in range(1, nz)]
    y_peers = [(dp, at_ep(nz, lax.rem(y + k, ny), z, core)) for k in range(1, ny)]
    x_peers = [(lax.rem(dp + k, n_dp), me) for k in range(1, n_dp)]
    right, left = (lax.rem(dp + 1, n_dp), me), (lax.rem(dp + n_dp - 1, n_dp), me)
    share, twin = me // repeat, lax.rem(me, repeat)
    share_peers = [
        (dp, lax.rem(share + k, n_shares) * repeat + twin) for k in range(1, n_shares)
    ]

    barrier = pltpu.get_barrier_semaphore()

    def greet(k, carry):
        pl.semaphore_signal(
            barrier, inc=1, device_id=(dp, lax.rem(me + k, ep)), device_id_type=MESH
        )
        return carry

    lax.fori_loop(1, ep, greet, 0)
    for peer in x_peers:
        pl.semaphore_signal(barrier, inc=1, device_id=peer, device_id_type=MESH)
    fetches = [
        pltpu.make_async_copy(source, target, weight_sems.at[k])
        for k, (source, target) in enumerate(
            ((w_gate_hbm, w_gate), (w_up_hbm, w_up), (w_down_hbm, w_down))
        )
    ]
    for fetch in fetches:
        fetch.start()

    local = tok_ref[...]
    router = router_ref[...]
    tok_all[me] = local
    cot_all[me] = cot_ref[...]
    wide = local.astype(f32)
    inverse_local = 1.0 / jnp.sqrt(jnp.sum(wide * wide, axis=1, keepdims=True) + eps_norm)
    router_wide = router.astype(f32)
    square = jnp.sum(router_wide * router_wide, axis=1, keepdims=True) + eps_norm
    square_row = jnp.broadcast_to(square, (experts, LANES)).T[0:1, :]
    inner = lax.dot_general(local, router, contract_last, preferred_element_type=f32)
    logits = cos_scale * inner * inverse_local / jnp.sqrt(square_row)
    ids = lax.broadcasted_iota(jnp.int32, (count, experts), 1).astype(f32)
    routes = assign_ref[...].astype(f32).T
    named = jnp.zeros((count, experts), f32)
    for k in range(routes.shape[1]):
        named = jnp.where(routes[:, k : k + 1] == ids, 1.0, named)
    start_kernel = jnp.exp(logits)
    signed = jnp.where(named > 0.0, -start_kernel, start_kernel)
    meta[core, mine] = jnp.concatenate([signed[: count // 2], signed[count // 2 :]], axis=1)

    pl.semaphore_wait(barrier, ep - 1 + n_dp - 1)

    def meta_copy(n, block, blocks, peer, c=core):
        ref = meta.at[c, pl.ds(block, blocks)]
        return pltpu.make_async_remote_copy(
            src_ref=ref, dst_ref=ref, send_sem=meta_send.at[n], recv_sem=meta_recv.at[n],
            device_id=peer, device_id_type=MESH,
        )

    meta_copies = [meta_copy(k, mine, 1, p) for k, p in enumerate(z_peers)]
    for copy in meta_copies:
        copy.start()

    ends = {
        ("z", 1): (dp, at_ep(nz, y, lax.rem(z + 1, nz), core)),
        ("z", -1): (dp, at_ep(nz, y, lax.rem(z + nz - 1, nz), core)),
        ("y", 1): (dp, at_ep(nz, lax.rem(y + 1, ny), z, core)),
        ("y", -1): (dp, at_ep(nz, lax.rem(y + ny - 1, ny), z, core)),
        ("mate", 0): mate,
    }

    def view(which, dy, dz, part, c):
        block = at_ep(nz, lax.rem(y - dy + 2 * ny, ny), lax.rem(z - dz + 2 * nz, nz), c)
        first, rows = (0, count) if part is None else (part * (count // 2), count // 2)
        ref, column, columns_held = pieces_of(width)[which]
        held = (tok_all, cot_all)[ref]
        return held.at[block, pl.ds(first, rows), pl.ds(column, columns_held)]

    def block_copy(n, ref, end):
        return pltpu.make_async_remote_copy(
            src_ref=ref, dst_ref=ref, send_sem=block_sends.at[n], recv_sem=block_recvs.at[n],
            device_id=ends[end], device_id_type=MESH,
        )

    gather_copies, mate_arrivals = [], []

    def run(step):
        arrival, step_sends = step
        if arrival is not None:
            n, which, dy, dz, part = arrival
            block_copy(n, view(which, dy, dz, part, core), ("z", 1)).wait_recv()
        for n, which, dy, dz, part, link, sign in step_sends:
            copy = block_copy(n, view(which, dy, dz, part, core), (link, sign))
            copy.start()
            gather_copies.append(copy)
            if link == "mate":
                mate_arrivals.append((n, which, dy, dz, part))

    steps = plan_of(ny, nz, width)[0]

    def compact(held, rows_ref, g):
        blocks = held[g * per_group : (g + 1) * per_group].reshape(GROUP, width)
        rows_ref[g * slots : (g + 1) * slots, :] = jnp.dot(
            pick[g], blocks, preferred_element_type=f32
        ).astype(bf16)

    row_step = min(256, ep * SLOTS)
    unit_step = min(256, hidden_units)
    row_steps = ep * SLOTS // row_step
    expert_steps = row_steps * (hidden_units // unit_step)

    def tile(i):
        row, unit = i % row_steps * row_step, i // row_steps * unit_step
        return slice(row, row + row_step), slice(unit, unit + unit_step)

    def forward(i):
        rows, units = tile(i)
        gate_linear = jnp.dot(rows_tok[rows, :], w_gate[:, units], preferred_element_type=f32)
        up_linear = jnp.dot(rows_tok[rows, :], w_up[:, units], preferred_element_type=f32)
        gate_all[rows, units] = gate_linear
        up_all[rows, units] = up_linear
        product = gate_linear * jax.nn.sigmoid(gate_linear) * up_linear
        weighted_rows[rows, units] = (rows_gate[rows, :] * product).astype(bf16)

    def norms(g):
        values = tok_all[g * per_group : (g + 1) * per_group].reshape(GROUP, width).astype(f32)
        inverse = 1.0 / jnp.sqrt(jnp.sum(values * values, axis=1, keepdims=True) + eps_norm)
        totals[ITERS + 1 : ITERS + 2, g * GROUP : (g + 1) * GROUP] = jnp.broadcast_to(
            inverse, (GROUP, LANES)
        ).T[0:1, :]

    def mates(wanted):
        for n, which, dy, dz, part in mate_arrivals:
            if pieces_of(width)[which][0] == wanted:
                block_copy(n, view(which, dy, dz, part, 1 - core), ("mate", 0)).wait_recv()

    def fetched():
        for fetch in fetches:
            fetch.wait()

    token_work = [functools.partial(compact, tok_all, rows_tok, g) for g in range(groups)]
    token_work += [fetched]
    token_work += [functools.partial(forward, i) for i in range(expert_steps)]
    token_work += [functools.partial(norms, g) for g in range(groups)]
    all_work = len(token_work)
    tokens_in = max(
        at for at, step in enumerate(steps) if pieces_of(width)[step[0][1] if step[0] else 0][0] == 0
    )
    first, second = tokens_in // 6, tokens_in // 3
    third, fourth = tokens_in // 2, tokens_in * 2 // 3
    ready = min(tokens_in + 4, len(steps) - 1)
    for at, step in enumerate(steps):
        if at == first:
            for k in range(nz - 1):
                meta_copy(k, y * nz + lax.rem(z - 1 - k + nz, nz), 1, mate).wait_recv()
            for k, peer in enumerate(y_peers):
                meta_copies.append(meta_copy(nz - 1 + k, y * nz, nz, peer))
                meta_copies[-1].start()
        if at == second:
            for k in range(ny - 1):
                block = lax.rem(y - 1 - k + ny, ny) * nz
                meta_copy(nz - 1 + k, block, nz, mate).wait_recv()
            meta_copies.append(meta_copy(nz + ny - 2, 0, ny * nz, mate))
            meta_copies[-1].start()
        if at == third:
            meta_copy(nz + ny - 2, 0, ny * nz, mate, 1 - core).wait_recv()
            tokens_down = lax.broadcasted_iota(jnp.int32, (count, count), 0)
            tokens_across = lax.broadcasted_iota(jnp.int32, (count, count), 1)
            sooner = jnp.where(tokens_across < tokens_down, 1.0, 0.0).astype(bf16)
            rank = jnp.dot(sooner, named.astype(bf16), preferred_element_type=f32)
            slot_of = jnp.where(named > 0.0, rank, -1.0).astype(bf16)
            expert_down = lax.broadcasted_iota(jnp.int32, (experts, experts * SLOTS), 0)
            slot_across = lax.broadcasted_iota(jnp.int32, (experts, experts * SLOTS), 1)
            widen = jnp.where(slot_across // SLOTS == expert_down, 1.0, 0.0).astype(bf16)
            slot_wide = jnp.dot(slot_of, widen, preferred_element_type=f32)
            across = lax.broadcasted_iota(jnp.int32, (count, experts * SLOTS), 1)
            slots_ref[...] = jnp.where(
                slot_wide == lax.rem(across, SLOTS).astype(f32), 1.0, 0.0
            ).astype(bf16)
        if at == fourth:
            balance(meta, kernels, columns, totals, marks, per_group)
            held = marks[pl.ds(me, 1), :] < 0.0
            kernel = jnp.where(held, kernels[ITERS, pl.ds(me, 1), :], 0.0)
            row_mask[...] = jnp.where(held, 1.0, 0.0)
            row_gate[...] = (kernel / totals[ITERS : ITERS + 1, :]).astype(bf16).astype(f32)
            before = lax.broadcasted_iota(jnp.int32, (GROUP, GROUP), 0)
            after = lax.broadcasted_iota(jnp.int32, (GROUP, GROUP), 1)
            earlier = jnp.where(
                (before < after) & (before // count == after // count), 1.0, 0.0
            ).astype(bf16)
            slot_ids = lax.broadcasted_iota(jnp.int32, (slots, GROUP), 0).astype(f32)
            base = (lax.broadcasted_iota(jnp.int32, (1, GROUP), 1) // count * SLOTS).astype(f32)
            for g in range(groups):
                mask = row_mask[:, g * GROUP : (g + 1) * GROUP]
                place_in = jnp.dot(
                    jnp.broadcast_to(mask, (8, GROUP)).astype(bf16), earlier,
                    preferred_element_type=f32,
                )[0:1]
                target = jnp.where(mask > 0.0, base + place_in, -1.0)
                chosen = jnp.where(slot_ids == target, 1.0, 0.0)
                rows_gate[g * slots : (g + 1) * slots, :] = jnp.sum(
                    chosen * row_gate[:, g * GROUP : (g + 1) * GROUP], axis=1, keepdims=True
                )
                pick[g] = chosen.astype(bf16)
        if at == ready:
            mates(0)
        if at > ready:
            done = all_work - len(token_work)
            due = all_work * (at - ready) // (len(steps) - 1 - ready) - done
            for work in token_work[:due]:
                work()
            token_work = token_work[due:]
        run(step)
    for work in token_work:
        work()
    mates(1)
    for g in range(groups):
        compact(cot_all, rows_cot, g)

    started = []
    across_table = width // hidden_units

    def buffer(n):
        if n < 2:
            return spare.at[n]
        block, column = (n - 2) // across_table, (n - 2) % across_table
        return cot_all.at[
            pl.ds(block * chunk_blocks, chunk_blocks),
            :,
            pl.ds(column * hidden_units, hidden_units),
        ]

    def far_buffer(a, side):
        return buffer(a * 2 + side)

    def near_buffer(a, side, half):
        return buffer(6 + a * 4 + side * 2 + half)

    def copy_of(n, ref, peer):
        return pltpu.make_async_remote_copy(
            src_ref=ref, dst_ref=ref, send_sem=sends.at[n], recv_sem=recvs.at[n],
            device_id=peer, device_id_type=MESH,
        )

    def start(copy):
        copy.start()
        started.append(copy)

    def far_copy(a, side):
        return pltpu.make_async_remote_copy(
            src_ref=far_buffer(a, side), dst_ref=got_far.at[a, side],
            send_sem=far_sends.at[a, side], recv_sem=far_recvs.at[a, side],
            device_id=(right, left)[side], device_id_type=MESH,
        )

    def near_copy(a, side, half):
        return pltpu.make_async_remote_copy(
            src_ref=near_buffer(a, side, half), dst_ref=got_near.at[a, side, half],
            send_sem=near_sends.at[a, side, half], recv_sem=near_recvs.at[a, side, half],
            device_id=(right, left)[side], device_id_type=MESH,
        )

    pairs = ((rows_cot, weighted_rows), (rows_tok, up_delta), (rows_tok, gate_delta))
    outs = (down_out, up_out, gate_out)
    arrays = range(3)

    def gradient(a, away, half):
        block = lax.rem(dp + away, n_dp)
        start_row = pl.multiple_of(block * (2 * chunk) + half * chunk, chunk)
        left_rows, right_rows = pairs[a]
        return lax.dot_general(
            left_rows[:, pl.ds(start_row, chunk)], right_rows[...], contract_first,
            preferred_element_type=f32,
        )

    def put(ref, value):
        ref[...] = value.astype(bf16).reshape(chunk_blocks, count, hidden_units)

    def far(a):
        for side in range(2):
            put(far_buffer(a, side), gradient(a, 2, side))
            start(far_copy(a, side))

    def near_plain(a):
        for side in range(2):
            put(near_buffer(a, side, 1 - side), gradient(a, (1, n_dp - 1)[side], 1 - side))
            start(near_copy(a, side, 1 - side))

    def near_joined(a):
        for side in range(2):
            mixed = gradient(a, (1, n_dp - 1)[side], side)
            far_copy(a, side).wait_recv()
            put(
                near_buffer(a, side, side),
                mixed + got_far[a, side].reshape(chunk, hidden_units).astype(f32),
            )
            start(near_copy(a, side, side))

    if ring:
        far(0)

    gate_grad[...] = jnp.zeros_like(gate_grad)

    def expert(i, carry):
        rows = pl.ds(pl.multiple_of(lax.rem(i, row_steps) * row_step, row_step), row_step)
        units = pl.ds(pl.multiple_of(i // row_steps * unit_step, unit_step), unit_step)
        raw_back = jnp.dot(rows_cot[rows, :], w_down[:, units], preferred_element_type=f32)
        gate_linear = gate_all[rows, units]
        up_linear = up_all[rows, units]
        sigmoid_gate = jax.nn.sigmoid(gate_linear)
        activation = gate_linear * sigmoid_gate
        product = activation * up_linear
        gate_grad[rows, :] += jnp.sum(
            raw_back * product.astype(bf16).astype(f32), axis=1, keepdims=True
        )
        scaled_back = rows_gate[rows, :] * raw_back
        up_delta[rows, units] = (scaled_back * activation).astype(bf16)
        gate_delta[rows, units] = (
            scaled_back * up_linear * sigmoid_gate * (1.0 + gate_linear * (1.0 - sigmoid_gate))
        ).astype(bf16)
        return carry

    lax.fori_loop(0, expert_steps, expert, 0)
    for copy in [*meta_copies, *gather_copies]:
        copy.wait_send()

    for g in range(groups):
        held = gate_grad[g * slots : (g + 1) * slots, :].astype(bf16).astype(f32)
        table[mine, core, g : g + 1, :] = jnp.sum(
            held * pick[g].astype(f32), axis=0, keepdims=True
        )
    n = 0

    def part(chip, chips):
        return table.at[pl.ds(chip, chips)]

    start(copy_of(n, table.at[mine, core], mate))
    if ring:
        far(1)
    copy_of(n, table.at[mine, 1 - core], mate).wait_recv()
    n += 1
    for k, peer in enumerate(z_peers):
        start(copy_of(n + k, part(mine, 1), peer))
    if ring:
        far(2)
    for k in range(nz - 1):
        copy_of(n + k, part(y * nz + lax.rem(z - 1 - k + nz, nz), 1), mate).wait_recv()
    n += nz - 1
    for k, peer in enumerate(y_peers):
        start(copy_of(n + k, part(y * nz, nz), peer))

    pieces = 4
    rows_each = ep // pieces

    def rows_back(q, carry):
        rows = pl.ds(pl.multiple_of(q * rows_each * SLOTS, rows_each * SLOTS), rows_each * SLOTS)
        value = lax.dot_general(
            gate_delta[rows, :], w_gate[...], contract_last, preferred_element_type=f32
        ) + lax.dot_general(up_delta[rows, :], w_up[...], contract_last, preferred_element_type=f32)
        route_back[pl.ds(q * rows_each, rows_each)] = value.astype(bf16).reshape(
            rows_each, SLOTS, width
        )
        return carry

    lax.fori_loop(0, pieces, rows_back, 0)

    def row_copy(k, from_block, to_block, peer):
        return pltpu.make_async_remote_copy(
            src_ref=route_back.at[from_block], dst_ref=back_rows.at[to_block],
            send_sem=row_sends.at[k], recv_sem=row_recvs.at[k],
            device_id=(dp, peer), device_id_type=MESH,
        )

    def send_rows(k, carry):
        peer = lax.rem(me + k, ep)
        row_copy(k, peer, me, peer).start()
        return carry

    lax.fori_loop(1, ep, send_rows, 0)
    back_rows[me] = route_back[me]
    if ring:
        near_plain(0)

    for k in range(ny - 1):
        copy_of(n + k, part(lax.rem(y - 1 - k + ny, ny) * nz, nz), mate).wait_recv()
    n += ny - 1

    for g in range(groups):
        both = table[:, :, g, :]
        grad[:, g * GROUP : (g + 1) * GROUP] = both.reshape(experts, GROUP)
    inverse_token = totals[ITERS + 1 : ITERS + 2, :]
    picked_sum = totals[ITERS : ITERS + 1, :]
    member = marks[...] < 0.0
    route = jnp.where(member, grad[...], 0.0)
    gates = jnp.where(member, kernels[ITERS], 0.0) / picked_sum
    grad[...] = jnp.where(
        member, (route - jnp.sum(route * gates, axis=0, keepdims=True)) / picked_sum, 0.0
    )
    for s in reversed(range(ITERS)):
        kernel = kernels[s + 1]
        row = totals[s : s + 1, :]
        column = columns[s][:, 0:1]
        slope = grad[...]
        slope = (slope - jnp.sum(slope * kernel, axis=0, keepdims=True)) / row
        moment = jnp.sum(slope * (kernel * row), axis=1, keepdims=True)
        grad[...] = (slope - moment) / column
    logit_grad = grad[...] * kernels[0]
    weighted = logit_grad * jnp.log(kernels[0])
    turn = logit_grad * (cos_scale * inverse_token) / jnp.sqrt(square)
    spread[:experts, :] = turn
    spread[experts:, :] = jnp.broadcast_to(
        jnp.sum(weighted, axis=0, keepdims=True) * inverse_token * inverse_token,
        (spread.shape[0] - experts, total),
    )

    own_lanes = pl.ds(pl.multiple_of(share * LANES, LANES), LANES)
    features = tok_all[:, :, own_lanes].reshape(total, LANES)
    product = jnp.dot(
        jnp.concatenate(split_three(turn), axis=0), features, preferred_element_type=f32
    )
    product = product[:experts] + product[experts : 2 * experts] + product[2 * experts :]
    own_router = router_ref[:, own_lanes].astype(f32)
    parts[dp] = product - own_router * (jnp.sum(weighted, axis=1, keepdims=True) / square)
    for k, peer in enumerate(x_peers):
        start(copy_of(n + k, parts.at[dp], peer))

    if ring:
        for a in (1, 2):
            near_plain(a)
        for a in arrays:
            near_joined(a)

    turned[...] = spread[:, pl.ds(pl.multiple_of(me * count // LANES * LANES, LANES), LANES)].T
    own = turned[pl.ds(pl.multiple_of(lax.rem(me, LANES // count) * count, count), count), :]
    back = jnp.zeros((count, width), f32)
    for term in split_three(own[:, :experts]):
        back += jnp.dot(term, router, preferred_element_type=f32)
    back -= tok_ref[...].astype(f32) * own[:, experts : experts + 1]

    for k in range(n_dp - 1):
        copy_of(n + k, parts.at[lax.rem(dp - 1 - k + n_dp, n_dp)], mate).wait_recv()
    n += n_dp - 1
    summed = parts[0]
    for k in range(1, n_dp):
        summed += parts[k]
    shares[share] = summed
    for k, peer in enumerate(share_peers):
        start(copy_of(n + k, shares.at[share], peer))

    def got_rows(k, carry):
        block = lax.rem(me - k + ep, ep)
        row_copy(k, block, block, block).wait_recv()
        return carry

    lax.fori_loop(1, ep, got_rows, 0)
    tokens_out[...] = (
        back
        + jnp.dot(
            slots_ref[...], back_rows[...].reshape(ep * SLOTS, width), preferred_element_type=f32
        )
    ).astype(bf16)

    for k in range(n_shares - 1):
        copy_of(n + k, shares.at[lax.rem(share - 1 - k + n_shares, n_shares)], mate).wait_recv()
    for k in range(n_shares):
        router_out[:, k * LANES : (k + 1) * LANES] = shares[k]

    def finish(a, half):
        value = gradient(a, 0, half)
        if ring:
            for side in range(2):
                near_copy(a, side, half).wait_recv()
                value += got_near[a, side, half].reshape(chunk, hidden_units).astype(f32)
        staged[a, half] = value.astype(bf16)
        copy = pltpu.make_async_copy(
            staged.at[a, half], outs[a].at[pl.ds(half * chunk, chunk)], out_sems.at[a, half]
        )
        copy.start()
        return copy

    written = [finish(a, half) for a in arrays for half in range(2)]

    def sent_rows(k, carry):
        peer = lax.rem(me + k, ep)
        row_copy(k, peer, me, peer).wait_send()
        return carry

    lax.fori_loop(1, ep, sent_rows, 0)
    for copy in started:
        copy.wait_send()
    for copy in written:
        copy.wait()


def copy_kernel(*refs):
    arrays = (len(refs) - 2) // 3
    sources, targets, stages = (refs[k * arrays : (k + 1) * arrays] for k in range(3))
    ins = [pltpu.make_async_copy(a, b, refs[-2].at[k]) for k, (a, b) in enumerate(zip(sources, stages))]
    outs = [pltpu.make_async_copy(a, b, refs[-1].at[k]) for k, (a, b) in enumerate(zip(stages, targets))]
    for copy in ins:
        copy.start()
    for arrived, copy in zip(ins, outs):
        arrived.wait()
        copy.start()
    for copy in outs:
        copy.wait()


def handed_on(arrays):
    anywhere = pl.BlockSpec(memory_space=pl.ANY)
    return pl.pallas_call(
        copy_kernel,
        out_shape=tuple(jax.ShapeDtypeStruct(a.shape, a.dtype) for a in arrays),
        in_specs=[anywhere] * len(arrays),
        out_specs=(anywhere,) * len(arrays),
        scratch_shapes=[
            *(pltpu.VMEM(a.shape, a.dtype) for a in arrays),
            pltpu.SemaphoreType.DMA((len(arrays),)),
            pltpu.SemaphoreType.DMA((len(arrays),)),
        ],
    )(*arrays)


def per_device(ep, n_dp, tokens, cotangent, assign, w_router, w_gate, w_up, w_down):
    ny, nz = torus_of(ep)
    _, count, width = tokens.shape
    experts = w_router.shape[1]
    hidden_units = w_gate.shape[2]
    total = ep * count
    groups = total // GROUP
    n_shares = width // LANES
    rows = ep * SLOTS
    chunk = width // n_dp // 2
    copies = 1 + nz - 1 + ny - 1 + n_dp - 1 + n_shares - 1
    blocks = plan_of(ny, nz, width)[1]
    shape, vmem_array, dma = jax.ShapeDtypeStruct, pltpu.VMEM, pltpu.SemaphoreType.DMA
    vmem = pl.BlockSpec(memory_space=pltpu.VMEM)
    anywhere = pl.BlockSpec(memory_space=pl.ANY)
    gradient = shape((2 * chunk, hidden_units), bf16)
    small = nz + ny - 1
    outs = pl.pallas_call(
        functools.partial(moe_kernel, ep, n_dp),
        out_shape=(
            shape((count, width), bf16),
            shape((experts, width), f32),
            gradient,
            gradient,
            gradient,
        ),
        in_specs=[vmem] * 4 + [anywhere] * 3,
        out_specs=(vmem, vmem, anywhere, anywhere, anywhere),
        scratch_shapes=[
            vmem_array((ep, count, width), bf16),
            vmem_array((ep, count, width), bf16),
            vmem_array((2, ny * nz, count // 2, 2 * experts), f32),
            vmem_array((rows, width), bf16),
            vmem_array((rows, width), bf16),
            vmem_array((rows, 1), f32),
            vmem_array((rows, 1), f32),
            vmem_array((rows, hidden_units), bf16),
            vmem_array((rows, hidden_units), bf16),
            vmem_array((rows, hidden_units), bf16),
            vmem_array((width, hidden_units), bf16),
            vmem_array((width, hidden_units), bf16),
            vmem_array((width, hidden_units), bf16),
            vmem_array((1, total), f32),
            vmem_array((1, total), f32),
            vmem_array((groups, GROUP // count * SLOTS, GROUP), bf16),
            vmem_array((ITERS + 1, experts, total), f32),
            vmem_array((ITERS, experts, LANES), f32),
            vmem_array((8, total), f32),
            vmem_array((experts, total), f32),
            vmem_array((count, experts * SLOTS), bf16),
            vmem_array((rows, hidden_units), f32),
            vmem_array((rows, hidden_units), f32),
            vmem_array((2, chunk // count, count, hidden_units), bf16),
            vmem_array((3, 2, chunk, hidden_units), bf16),
            vmem_array((ny * nz, 2, groups, GROUP), f32),
            vmem_array((experts, total), f32),
            vmem_array((LANES, total), f32),
            vmem_array((LANES, LANES), f32),
            vmem_array((n_dp, experts, LANES), f32),
            vmem_array((n_shares, experts, LANES), f32),
            vmem_array((ep, SLOTS, width), bf16),
            vmem_array((ep, SLOTS, width), bf16),
            vmem_array((3, 2, chunk // count, count, hidden_units), bf16),
            vmem_array((3, 2, 2, chunk // count, count, hidden_units), bf16),
            dma((small,)),
            dma((small,)),
            dma((blocks,)),
            dma((blocks,)),
            dma((copies,)),
            dma((copies,)),
            dma((ep,)),
            dma((ep,)),
            dma((3, 2)),
            dma((3, 2)),
            dma((3, 2, 2)),
            dma((3, 2, 2)),
            dma((3,)),
            dma((3, 2)),
        ],
        compiler_params=pltpu.CompilerParams(
            collective_id=1, has_side_effects=True, vmem_limit_bytes=60 * 2**20
        ),
    )(tokens[0], cotangent[0], assign[0].T, w_router.T, w_gate[0], w_up[0], w_down[0])
    grad_tokens, grad_router, grad_gate, grad_up, grad_down = handed_on(outs)
    return grad_tokens[None], grad_router.T, grad_gate[None], grad_up[None], grad_down[None]


def solution(mesh):
    return jax.shard_map(
        functools.partial(per_device, mesh.shape["ep"], mesh.shape["dp"]),
        mesh=mesh,
        in_specs=(
            P("dp", "ep", None),
            P("dp", "ep", None),
            P("dp", "ep", None),
            P(),
            P("ep", None, None),
            P("ep", None, None),
            P("ep", None, None),
        ),
        out_specs=(
            P("dp", "ep", None),
            P(),
            P("ep", "dp", None),
            P("ep", "dp", None),
            P("ep", "dp", None),
        ),
        check_vma=False,
    )
```
